256 devices in a mesh: row: 16 (over x, y), col: 16 (over z, core).
Axes of the slice: x: 4, y: 4, z: 8, core: 2. Of those that a mesh axis runs over, the one named last changes fastest.
Arguments:
- tokens: bfloat16 [512, 16384], P('col', 'row'), may hold values from -6 to 6
- cotangent: bfloat16 [512, 16384], P('col', 'row'), may hold values from -6 to 6
- gate_weight: bfloat16 [16384, 26624], P('row', 'col'), may hold values from -0.046875 to 0.046875
- up_weight: bfloat16 [16384, 26624], P('row', 'col'), may hold values from -0.046875 to 0.046875
- down_weight: bfloat16 [26624, 16384], P('col', 'row'), may hold values from -0.0390625 to 0.0390625
Outputs:
- output: bfloat16 [512, 16384], P('col', 'row')
- input_grad: bfloat16 [512, 16384], P('col', 'row')
The draws below stay inside these ranges and needn't reach their ends.
All inputs are finite; a program needn't handle non-finite values.
Results may differ from the reference program's by a relative error of at most 0.005.
Values may be sent and summed in bfloat16 or wider, within the bound.
A program may use at most 128 MiB of HBM per device.

```python
import jax
import jax.numpy as jnp
from jax import lax

D = 16384
FF = 26624
TOKENS = 512


def block_levels(own_key, extent, split, smallest, high):
    level, own = 1.0, jax.random.fold_in(own_key, 6)
    for position, blocks in split:
        heights = jnp.exp(jax.random.uniform(jax.random.fold_in(own, position), (blocks,), jnp.float32, smallest / len(split), high / len(split)))
        level = level * jnp.repeat(heights, extent[position] // blocks).reshape([-1 if axis == position else 1 for axis in range(len(extent))])
    return level


def bell_draw(key, shape, scale, most, pieces=(), kind=jnp.bfloat16):
    values = scale * jax.random.normal(key, shape, jnp.float32)
    if pieces:
        values = values * block_levels(key, shape, pieces, -0.22, 0.18)
    return jnp.clip(values, -most, most).astype(kind)


def setup_inputs(seed: int = 0) -> dict:
    seeds = jax.random.split(jax.random.key(seed), 6)
    tokens = bell_draw(seeds[0], (TOKENS, D), 1.0, 6.0, ((0, 16), (1, 16)))
    cotangent = bell_draw(seeds[1], (TOKENS, D), 1.0, 6.0, ((0, 16), (1, 16)))
    gate_weight = bell_draw(seeds[2], (D, FF), D ** -0.5, 0.046875, ((0, 16), (1, 16)))
    up_weight = bell_draw(seeds[3], (D, FF), D ** -0.5, 0.046875, ((0, 16), (1, 16)))
    down_weight = bell_draw(seeds[4], (FF, D), FF ** -0.5, 0.0390625, ((0, 16), (1, 16)))
    return dict(tokens=tokens, cotangent=cotangent, gate_weight=gate_weight, up_weight=up_weight, down_weight=down_weight)


def transposed(left, right):
    return lax.dot_general(left, right, (((1,), (1,)), ((), ())), preferred_element_type=jnp.float32)


def reference(tokens, cotangent, gate_weight, up_weight, down_weight):
    gate = jnp.dot(tokens, gate_weight, preferred_element_type=jnp.float32)
    up = jnp.dot(tokens, up_weight, preferred_element_type=jnp.float32)
    sigmoid_gate = jax.nn.sigmoid(gate)
    hidden = (gate * sigmoid_gate * up).astype(jnp.bfloat16)
    output = jnp.dot(hidden, down_weight, preferred_element_type=jnp.float32).astype(jnp.bfloat16)
    hidden_grad = transposed(cotangent, down_weight)
    gate_grad = (hidden_grad * up * sigmoid_gate * (1.0 + gate * (1.0 - sigmoid_gate))).astype(jnp.bfloat16)
    up_grad = (hidden_grad * gate * sigmoid_gate).astype(jnp.bfloat16)
    input_grad = (transposed(gate_grad, gate_weight) + transposed(up_grad, up_weight)).astype(jnp.bfloat16)
    return output, input_grad
```

```python
import functools

import jax
import jax.numpy as jnp
from jax import lax
from jax.experimental import pallas as pl
from jax.experimental.pallas import tpu as pltpu
from jax.sharding import PartitionSpec as P

MESH = pl.DeviceIdType.MESH
NX, NY, NZ = 4, 4, 8
NB = NX * NY
HALF = 16
TILE = 256


def kernel(
    split,
    tokens,
    cotangent,
    gate_weight,
    up_weight,
    down_weight,
    output,
    input_grad,
    gu_w,
    down_w,
    seen,
    send1_p,
    send1_q,
    full_p,
    full_q,
    recv1_p,
    recv1_q,
    send2_p,
    send2_q,
    recv2_p,
    recv2_q,
    own2_p,
    own2_q,
    gate_up,
    hidden,
    grads,
    acc,
    pair,
    zsend,
    zrecv,
    load_sem,
    seen_s,
    seen_r,
    share_s,
    share_r,
    rs1_s,
    rs1_r,
    rs2_s,
    rs2_r,
    ag1_s,
    ag1_r,
    ag2_s,
    ag2_r,
    pair_s,
    pair_r,
    z_s,
    z_r,
):
    width = gate_weight.shape[1]
    row, col = lax.axis_index("row"), lax.axis_index("col")
    x, y = row // NY, row % NY
    z, k = col // 2, col % 2

    def at(dx=0, dy=0, dz=0, dk=0):
        return (
            ((x + dx) % NX) * NY + (y + dy) % NY,
            ((z + dz) % NZ) * 2 + (k + dk) % 2,
        )

    def remote(src, dst, send, recv, device):
        return pltpu.make_async_remote_copy(
            src_ref=src,
            dst_ref=dst,
            send_sem=send,
            recv_sem=recv,
            device_id=device,
            device_id_type=MESH,
        )

    offset = (0, split)
    widths = (split, width - split)
    span1 = tuple(pl.ds(offset[o], widths[o]) for o in range(2))
    span2 = tuple(pl.ds(2 * offset[o], 2 * widths[o]) for o in range(2))

    loads = []
    for i, (src, dst) in enumerate(
        [(tokens.at[pl.ds(g * HALF, HALF)], seen.at[0, g, col]) for g in range(2)]
        + [(cotangent.at[pl.ds(g * HALF, HALF)], seen.at[1, g, col]) for g in range(2)]
        + [
            (src.at[:, span1[o]], gu_w.at[:, pl.ds(2 * offset[o] + p * widths[o], widths[o])])
            for o in range(2)
            for p, src in enumerate((gate_weight, up_weight))
        ]
        + [(down_weight, down_w)]
    ):
        loads.append(pltpu.make_async_copy(src, dst, load_sem.at[i]))

    barrier = pltpu.get_barrier_semaphore()
    friends = (
        [at(dx=d) for d in range(1, NX)]
        + [at(dy=d) for d in range(1, NY)]
        + [at(dz=d) for d in range(1, NZ)]
        + [at(dk=1)]
    )
    for friend in friends:
        pl.semaphore_signal(barrier, inc=1, device_id=friend, device_id_type=MESH)
    for load in loads:
        load.start()
    pl.semaphore_wait(barrier, len(friends))

    pending = []

    def go(copy):
        copy.start()
        pending.append(copy)

    def own_block(t, g):
        return (tokens, cotangent)[t].at[pl.ds(g * HALF, HALF)]

    def gather_copies(t, g):
        return [
            remote(
                own_block(t, g),
                seen.at[t, g, col],
                seen_s.at[t, g, d - 1],
                seen_r.at[t, g, d - 1],
                at(dz=d),
            )
            for d in range(1, NZ)
        ]

    def share_copy(t, g, d):
        block = ((z - d) % NZ) * 2 + k
        src = own_block(t, g) if d == 0 else seen.at[t, g, block]
        return remote(
            src, seen.at[t, g, block], share_s.at[t, g, d], share_r.at[t, g, d], at(dk=1)
        )

    def gather_start(t, g):
        order = sorted(range(1, NZ), key=lambda d: -min(d, NZ - d))
        copies = gather_copies(t, g)
        for d in order:
            go(copies[d - 1])
        go(share_copy(t, g, 0))

    def gather_finish(t, g):
        copies = gather_copies(t, g)
        for d in sorted(range(1, NZ), key=lambda d: min(d, NZ - d)):
            copies[d - 1].wait_recv()
            go(share_copy(t, g, d))
        for d in range(NZ):
            share_copy(t, g, d).wait_recv()
        loads[2 * t + g].wait()

    def product(left, weight, turned, full, send, g, start, extent):
        def tile(first, size):
            cols = pl.ds(first, size)
            if turned:
                term = lax.dot_general(
                    left, weight[cols, :], (((1,), (1,)), ((), ())),
                    preferred_element_type=jnp.float32,
                )
            else:
                term = jnp.dot(left, weight[:, cols], preferred_element_type=jnp.float32)
            term = term.reshape(NX, NY, HALF, size)
            full[g, :, :, :, cols] = term
            send[g, :, :, :, cols] = term.astype(jnp.bfloat16)

        count = extent // TILE

        @pl.loop(0, count)
        def _(n):
            tile(pl.multiple_of(start + n * TILE, 128), TILE)

        if extent % TILE:
            tile(start + count * TILE, extent % TILE)

    kinds = (
        (span2, full_p, send1_p, recv1_p, send2_p, recv2_p, own2_p),
        (span1, full_q, send1_q, recv1_q, send2_q, recv2_q, own2_q),
    )

    def rs1_copies(q, g, o):
        span, _, send1, recv1, _, _, _ = kinds[q]
        copies = []
        for d in range(1, NX):
            if o == 0:
                src, device = send1.at[g, (x + d) % NX, :, :, span[o]], at(dx=d)
            else:
                src, device = send1.at[g, :, (y + d) % NY, :, span[o]], at(dy=d)
            copies.append(
                remote(
                    src,
                    recv1.at[g, d - 1, :, :, span[o]],
                    rs1_s.at[q, g, o, d - 1],
                    rs1_r.at[q, g, o, d - 1],
                    device,
                )
            )
        return copies

    def step_b(q, g, o):
        left = seen[q, g].reshape(NB * HALF, seen.shape[-1])
        if q == 0:
            product(left, gu_w, False, full_p, send1_p, g, 2 * offset[o], 2 * widths[o])
        else:
            product(left, down_w, True, full_q, send1_q, g, offset[o], widths[o])
        copies = rs1_copies(q, g, o)
        for d in (2, 1, 3):
            go(copies[d - 1])

    def rs2_copies(q, g, o):
        span, _, _, _, send2, recv2, _ = kinds[q]
        return [
            remote(
                send2.at[g, ((y if o == 0 else x) + d) % NX, :, span[o]],
                recv2.at[g, d - 1, :, span[o]],
                rs2_s.at[q, g, o, d - 1],
                rs2_r.at[q, g, o, d - 1],
                at(dy=d) if o == 0 else at(dx=d),
            )
            for d in range(1, NX)
        ]

    def step_s1(q, g, o):
        span, full, _, recv1, send2, _, own2 = kinds[q]
        for copy in rs1_copies(q, g, o):
            copy.wait_recv()

        def total(i):
            mine = full[g, x, i, :, span[o]] if o == 0 else full[g, i, y, :, span[o]]
            for d in range(NX - 1):
                mine += recv1[g, d, i, :, span[o]].astype(jnp.float32)
            return mine

        for i in range(NX):
            send2[g, i, :, span[o]] = total(i).astype(jnp.bfloat16)
        own2[g, :, span[o]] = total(y if o == 0 else x)
        for copy in rs2_copies(q, g, o):
            go(copy)

    def ag_bufs(q):
        return (hidden, span1) if q == 0 else (grads, span2)

    def ag1_copies(q, g, o):
        buf, span = ag_bufs(q)
        mine = buf.at[g, x, y, :, span[o]]
        return [
            remote(
                mine,
                mine,
                ag1_s.at[q, g, o, d - 1],
                ag1_r.at[q, g, o, d - 1],
                at(dy=d) if o == 0 else at(dx=d),
            )
            for d in range(1, NX)
        ]

    def ag2_copies(q, g, o):
        buf, span = ag_bufs(q)
        mine = buf.at[g, x, :, :, span[o]] if o == 0 else buf.at[g, :, y, :, span[o]]
        return [
            remote(
                mine,
                mine,
                ag2_s.at[q, g, o, d - 1],
                ag2_r.at[q, g, o, d - 1],
                at(dx=d) if o == 0 else at(dy=d),
            )
            for d in range(1, NX)
        ]

    def step_s2(q, g, o):
        span, _, _, _, _, recv2, own2 = kinds[q]
        for copy in rs2_copies(q, g, o):
            copy.wait_recv()
        total = own2[g, :, span[o]]
        for d in range(NX - 1):
            total += recv2[g, d, :, span[o]].astype(jnp.float32)
        first, second = (
            pl.ds(2 * offset[o], widths[o]),
            pl.ds(2 * offset[o] + widths[o], widths[o]),
        )
        if q == 0:
            gate_up[g, :, span[o]] = total
            gate, up = total[:, : widths[o]], total[:, widths[o] :]
            hidden[g, x, y, :, span1[o]] = (gate * jax.nn.sigmoid(gate) * up).astype(
                jnp.bfloat16
            )
        else:
            gate, up = gate_up[g, :, first], gate_up[g, :, second]
            sigmoid = jax.nn.sigmoid(gate)
            grads[g, x, y, :, first] = (
                total * up * sigmoid * (1.0 + gate * (1.0 - sigmoid))
            ).astype(jnp.bfloat16)
            grads[g, x, y, :, second] = (total * gate * sigmoid).astype(jnp.bfloat16)
        for copy in ag1_copies(q, g, o):
            go(copy)

    def step_g1(q, g, o):
        for copy in ag1_copies(q, g, o):
            copy.wait_recv()
        copies = ag2_copies(q, g, o)
        for d in (2, 1, 3):
            go(copies[d - 1])

    def pair_copy(t, g):
        return remote(
            acc.at[t, g, :, 1 - k],
            pair.at[t, g],
            pair_s.at[t, g],
            pair_r.at[t, g],
            at(dk=1),
        )

    def step_f(q, g):
        for o in range(2):
            for copy in ag2_copies(q, g, o):
                copy.wait_recv()
        buf, _ = ag_bufs(q)
        left = buf[g].reshape(NB * HALF, buf.shape[-1])

        @pl.loop(0, down_w.shape[1] // TILE)
        def _(n):
            cols = pl.ds(pl.multiple_of(n * TILE, TILE), TILE)
            if q == 0:
                term = jnp.dot(left, down_w[:, cols], preferred_element_type=jnp.float32)
            else:
                term = lax.dot_general(
                    left, gu_w[cols, :], (((1,), (1,)), ((), ())),
                    preferred_element_type=jnp.float32,
                )
            acc[q, g, :, :, :, cols] = term.reshape(NZ, 2, HALF, TILE)

        go(pair_copy(q, g))

    def z_copies(t, g):
        return [
            remote(
                zsend.at[t, g, (z + d) % NZ],
                zrecv.at[t, g, d - 1],
                z_s.at[t, g, d - 1],
                z_r.at[t, g, d - 1],
                at(dz=d),
            )
            for d in range(1, NZ)
        ]

    def step_z(t, g):
        pair_copy(t, g).wait_recv()

        @pl.loop(0, NZ)
        def _(i):
            zsend[t, g, i] = (acc[t, g, i, k] + pair[t, g, i]).astype(jnp.bfloat16)

        copies = z_copies(t, g)
        for d in sorted(range(1, NZ), key=lambda d: -min(d, NZ - d)):
            go(copies[d - 1])

    def step_out(t, g):
        total = acc[t, g, z, k] + pair[t, g, z]
        for d in range(1, NZ):
            z_copies(t, g)[d - 1].wait_recv()
            total += zrecv[t, g, d - 1].astype(jnp.float32)
        (output, input_grad)[t][pl.ds(g * HALF, HALF), :] = total.astype(jnp.bfloat16)

    def both(step, q, g):
        for o in range(2):
            step(q, g, o)

    gather_start(0, 0)
    gather_finish(0, 0)
    gather_start(0, 1)
    for load in loads[4:8]:
        load.wait()
    both(step_b, 0, 0)
    gather_finish(0, 1)
    gather_start(1, 0)
    both(step_b, 0, 1)
    both(step_s1, 0, 0)
    gather_finish(1, 0)
    gather_start(1, 1)
    loads[8].wait()
    both(step_b, 1, 0)
    both(step_s2, 0, 0)
    both(step_s1, 0, 1)
    gather_finish(1, 1)
    both(step_b, 1, 1)
    both(step_g1, 0, 0)
    both(step_s2, 0, 1)
    both(step_s1, 1, 0)
    step_f(0, 0)
    both(step_g1, 0, 1)
    both(step_s2, 1, 0)
    both(step_s1, 1, 1)
    step_z(0, 0)
    step_f(0, 1)
    both(step_g1, 1, 0)
    both(step_s2, 1, 1)
    step_z(0, 1)
    step_out(0, 0)
    both(step_g1, 1, 1)
    step_f(1, 0)
    step_out(0, 1)
    step_z(1, 0)
    step_f(1, 1)
    step_z(1, 1)
    step_out(1, 0)
    step_out(1, 1)
    for copy in pending:
        copy.wait_send()


def body(tokens, cotangent, gate_weight, up_weight, down_weight):
    rows, depth = tokens.shape
    width = gate_weight.shape[1]
    split = (width // 128 + 1) // 2 * 128
    bf16, f32, dma = jnp.bfloat16, jnp.float32, pltpu.SemaphoreType.DMA
    vmem = pltpu.VMEM
    assert rows == 2 * HALF
    scratch = [
        vmem((depth, 2 * width), bf16),
        vmem((width, depth), bf16),
        vmem((2, 2, 2 * NZ, HALF, depth), bf16),
        vmem((2, NX, NY, HALF, 2 * width), bf16),
        vmem((2, NX, NY, HALF, width), bf16),
        vmem((2, NX, NY, HALF, 2 * width), f32),
        vmem((2, NX, NY, HALF, width), f32),
        vmem((2, NX - 1, NX, HALF, 2 * width), bf16),
        vmem((2, NX - 1, NX, HALF, width), bf16),
        vmem((2, NX, HALF, 2 * width), bf16),
        vmem((2, NX, HALF, width), bf16),
        vmem((2, NX - 1, HALF, 2 * width), bf16),
        vmem((2, NX - 1, HALF, width), bf16),
        vmem((2, HALF, 2 * width), f32),
        vmem((2, HALF, width), f32),
        vmem((2, HALF, 2 * width), f32),
        vmem((2, NX, NY, HALF, width), bf16),
        vmem((2, NX, NY, HALF, 2 * width), bf16),
        vmem((2, 2, NZ, 2, HALF, depth), f32),
        vmem((2, 2, NZ, HALF, depth), f32),
        vmem((2, 2, NZ, HALF, depth), bf16),
        vmem((2, 2, NZ - 1, HALF, depth), bf16),
        dma((9,)),
        dma((2, 2, NZ - 1)),
        dma((2, 2, NZ - 1)),
        dma((2, 2, NZ)),
        dma((2, 2, NZ)),
    ]
    scratch += [dma((2, 2, 2, NX - 1)) for _ in range(8)]
    scratch += [dma((2, 2)), dma((2, 2)), dma((2, 2, NZ - 1)), dma((2, 2, NZ - 1))]
    shape = jax.ShapeDtypeStruct((rows, depth), bf16)
    return pl.pallas_call(
        functools.partial(kernel, split),
        name="swiglu_both_ways",
        out_shape=(shape, shape),
        in_specs=[pl.BlockSpec(memory_space=pl.ANY)] * 5,
        out_specs=(pl.BlockSpec(memory_space=pltpu.VMEM),) * 2,
        scratch_shapes=scratch,
        compiler_params=pltpu.CompilerParams(
            collective_id=0, has_side_effects=True, vmem_limit_bytes=60 << 20
        ),
    )(tokens, cotangent, gate_weight, up_weight, down_weight)


def solution(mesh):
    placed = (P("col", "row"), P("col", "row"), P("row", "col"), P("row", "col"), P("col", "row"))
    return jax.shard_map(
        body,
        mesh=mesh,
        in_specs=placed,
        out_specs=(P("col", "row"), P("col", "row")),
        check_vma=False,
    )
```

```python
import functools

import jax
import jax.numpy as jnp
from jax import lax
from jax.experimental import pallas as pl
from jax.experimental.pallas import tpu as pltpu
from jax.sharding import PartitionSpec as P

MESH = pl.DeviceIdType.MESH
NX, NY, NZ = 4, 4, 8
NB = NX * NY
HALF = 16
TILE = 256
GROUPS = (
    ((0, 2, -1, 0), (2, 2, 0, 0), (4, 2, 1, 0), (6, 1, 2, 0), (7, 1, -2, 0)),
    ((0, 1, 2, 1), (1, 1, -2, 1), (2, 2, 3, 0), (4, 2, -3, 0), (6, 2, 4, 0)),
)
NEAR, FAR = 0, 1
SEMAPHORES = {
    "seen": (2, 2, 5),
    "share": (2, 2, 5),
    "rs1": (2, 2, 2, 6),
    "rs2": (2, 2, 2, NX - 1),
    "ag1": (2, 2, 2, NX - 1),
    "ag2": (2, 2, 2, 6),
    "pair": (2, 2, 2),
    "z": (2, 2, 2, 5),
}
KINDS = tuple(SEMAPHORES)


def kernel(
    split,
    tokens,
    cotangent,
    gate_weight,
    up_weight,
    down_weight,
    both_out,
    gu_w,
    down_w,
    seen,
    send1_p,
    send1_q,
    full_p,
    full_q,
    recv1_p,
    recv1_q,
    relay_p,
    relay_q,
    send2_p,
    send2_q,
    recv2_p,
    recv2_q,
    own2_p,
    own2_q,
    gate_up,
    hidden,
    grads,
    acc,
    pair,
    zsend,
    zrecv,
    result,
    load_sem,
    *sems,
):
    width = gate_weight.shape[1]
    row, col = lax.axis_index("row"), lax.axis_index("col")
    x, y = row // NY, row % NY
    z, k = col // 2, col % 2

    def at(dx=0, dy=0, dz=0, dk=0):
        return (
            ((x + dx) % NX) * NY + (y + dy) % NY,
            ((z + dz) % NZ) * 2 + (k + dk) % 2,
        )

    def remote(src, dst, kind, index, device):
        send, recv = sems[2 * KINDS.index(kind)], sems[2 * KINDS.index(kind) + 1]
        return pltpu.make_async_remote_copy(
            src_ref=src,
            dst_ref=dst,
            send_sem=send.at[index],
            recv_sem=recv.at[index],
            device_id=device,
            device_id_type=MESH,
        )

    offset = (0, split)
    widths = (split, width - split)
    span1 = tuple(pl.ds(offset[o], widths[o]) for o in range(2))
    span2 = tuple(pl.ds(2 * offset[o], 2 * widths[o]) for o in range(2))

    loads = [
        pltpu.make_async_copy(src, dst, load_sem.at[i])
        for i, (src, dst) in enumerate(
            [(tokens, seen.at[0, NEAR, pl.ds(2, 2), k]), (cotangent, seen.at[1, NEAR, pl.ds(2, 2), k])]
            + [
                (
                    src.at[:, span1[o]],
                    gu_w.at[:, pl.ds(2 * offset[o] + p * widths[o], widths[o])],
                )
                for o in range(2)
                for p, src in enumerate((gate_weight, up_weight))
            ]
            + [(down_weight, down_w)]
        )
    ]

    barrier = pltpu.get_barrier_semaphore()
    friends = (
        [at(dx=d) for d in range(1, NX)]
        + [at(dy=d) for d in range(1, NY)]
        + [at(dz=d) for d in range(1, NZ)]
        + [at(dk=1)]
    )
    for friend in friends:
        pl.semaphore_signal(barrier, inc=1, device_id=friend, device_id_type=MESH)
    pl.semaphore_wait(barrier, len(friends))

    pending = []

    def go(copy):
        copy.start()
        pending.append(copy)

    def own_block(t, n, h):
        return (tokens, cotangent)[t].at[pl.ds(h, n)]

    def gather_copy(t, g, e):
        j, n, dz, h = GROUPS[g][e]
        return remote(
            own_block(t, n, h), seen.at[t, g, pl.ds(j, n), k], "seen", (t, g, e), at(dz=-dz)
        )

    def share_copy(t, g, e):
        j, n, dz, h = GROUPS[g][e]
        block = seen.at[t, g, pl.ds(j, n), k]
        src = own_block(t, n, h) if dz == 0 else block
        return remote(src, block, "share", (t, g, e), at(dk=1))

    def gather_start(t, g):
        for e, (_, _, dz, _) in enumerate(GROUPS[g]):
            go(gather_copy(t, g, e) if dz else share_copy(t, g, e))

    def gather_finish(t, g, then=None):
        runs = sorted(enumerate(GROUPS[g]), key=lambda run: abs(run[1][2]))
        for e, (_, _, dz, _) in runs:
            if dz:
                gather_copy(t, g, e).wait_recv()
                go(share_copy(t, g, e))
        if then is not None:
            gather_start(*then)
        for e, _ in runs:
            share_copy(t, g, e).wait_recv()

    def product(left, weight, turned, full, send, g, start, extent):
        def tile(first, size):
            cols = pl.ds(first, size)
            if turned:
                term = lax.dot_general(
                    left, weight[cols, :], (((1,), (1,)), ((), ())),
                    preferred_element_type=jnp.float32,
                )
            else:
                term = jnp.dot(left, weight[:, cols], preferred_element_type=jnp.float32)
            term = term.reshape(NX, NY, HALF, size)
            full[g, :, :, :, cols] = term
            send[g, :, :, :, cols] = term.astype(jnp.bfloat16)

        count = extent // TILE

        @pl.loop(0, count)
        def _(n):
            tile(pl.multiple_of(start + n * TILE, 128), TILE)

        if extent % TILE:
            tile(start + count * TILE, extent % TILE)

    kinds = (
        (span2, full_p, send1_p, recv1_p, relay_p, send2_p, recv2_p, own2_p),
        (span1, full_q, send1_q, recv1_q, relay_q, send2_q, recv2_q, own2_q),
    )
    low, high, whole = pl.ds(0, NX // 2), pl.ds(NX // 2, NX // 2), pl.ds(0, NX)

    def line(o, step):
        return (at(dx=step), (x + step) % NX) if o == 0 else (at(dy=step), (y + step) % NY)

    def part(buf, g, o, chunk, inner, cols):
        if o == 0:
            return buf.at[g, chunk, inner, :, cols]
        return buf.at[g, inner, chunk, :, cols]

    def rs1_copies(q, g, o):
        span, _, send1, recv1, relay, _, _, _ = kinds[q]
        (right, after), (left, before), (_, opposite) = line(o, 1), line(o, -1), line(o, 2)
        plan = [
            (right, opposite, low, relay.at[g, low, :, span[o]]),
            (left, opposite, high, relay.at[g, high, :, span[o]]),
            (right, after, high, recv1.at[g, 0, high, :, span[o]]),
            (left, before, low, recv1.at[g, 1, low, :, span[o]]),
            (right, after, low, recv1.at[g, 0, low, :, span[o]]),
            (left, before, high, recv1.at[g, 1, high, :, span[o]]),
        ]
        return [
            remote(part(send1, g, o, chunk, inner, span[o]), dst, "rs1", (q, g, o, n), device)
            for n, (device, chunk, inner, dst) in enumerate(plan)
        ]

    def step_b(q, g):
        left = seen[q, g].reshape(NB * HALF, seen.shape[-1])
        for o in range(2):
            if q == 0:
                product(left, gu_w, False, full_p, send1_p, g, 2 * offset[o], 2 * widths[o])
            else:
                product(left, down_w, True, full_q, send1_q, g, offset[o], widths[o])
            for copy in rs1_copies(q, g, o)[:2]:
                go(copy)
        for o in range(2):
            for copy in rs1_copies(q, g, o)[2:4]:
                go(copy)

    def step_r(q, g, o):
        span, full, send1, _, relay, _, _, _ = kinds[q]
        copies = rs1_copies(q, g, o)
        for side, blocks in enumerate((range(NX // 2), range(NX // 2, NX))):
            copies[side].wait_recv()
            _, chunk = line(o, 1 - 2 * side)
            for i in blocks:
                total = part(full, g, o, chunk, i, span[o])[...]
                total += relay[g, i, :, span[o]].astype(jnp.float32)
                part(send1, g, o, chunk, i, span[o])[...] = total.astype(jnp.bfloat16)
            go(copies[4 + side])

    def rs2_copies(q, g, o):
        span, _, _, _, _, send2, recv2, _ = kinds[q]
        return [
            remote(
                send2.at[g, ((y if o == 0 else x) + d) % NX, :, span[o]],
                recv2.at[g, d - 1, :, span[o]],
                "rs2",
                (q, g, o, d - 1),
                at(dy=d) if o == 0 else at(dx=d),
            )
            for d in range(1, NX)
        ]

    def step_s1(q, g, o):
        span, full, _, recv1, _, send2, _, own2 = kinds[q]
        for copy in rs1_copies(q, g, o)[2:]:
            copy.wait_recv()

        def total(i):
            mine = full[g, x, i, :, span[o]] if o == 0 else full[g, i, y, :, span[o]]
            for d in range(2):
                mine += recv1[g, d, i, :, span[o]].astype(jnp.float32)
            return mine

        for i in range(NX):
            send2[g, i, :, span[o]] = total(i).astype(jnp.bfloat16)
        own2[g, :, span[o]] = total(y if o == 0 else x)
        for copy in rs2_copies(q, g, o):
            go(copy)

    def ag_bufs(q):
        return (hidden, span1) if q == 0 else (grads, span2)

    def ag1_copies(q, g, o):
        buf, span = ag_bufs(q)
        mine = buf.at[g, x, y, :, span[o]]
        return [
            remote(
                mine,
                mine,
                "ag1",
                (q, g, o, d - 1),
                at(dy=d) if o == 0 else at(dx=d),
            )
            for d in range(1, NX)
        ]

    def ag2_copies(q, g, o):
        buf, span = ag_bufs(q)
        (right, _), (left, before), (_, mine), (_, after) = (
            line(o, 1),
            line(o, -1),
            line(o, 0),
            line(o, 1),
        )
        plan = [
            (right, mine, low),
            (left, mine, high),
            (right, mine, high),
            (left, mine, low),
            (right, before, low),
            (left, after, high),
        ]
        return [
            remote(
                part(buf, g, o, chunk, inner, span[o]),
                part(buf, g, o, chunk, inner, span[o]),
                "ag2",
                (q, g, o, n),
                device,
            )
            for n, (device, chunk, inner) in enumerate(plan)
        ]

    def step_s2(q, g, o):
        span, _, _, _, _, _, recv2, own2 = kinds[q]
        for copy in rs2_copies(q, g, o):
            copy.wait_recv()
        total = own2[g, :, span[o]]
        for d in range(NX - 1):
            total += recv2[g, d, :, span[o]].astype(jnp.float32)
        first, second = (
            pl.ds(2 * offset[o], widths[o]),
            pl.ds(2 * offset[o] + widths[o], widths[o]),
        )
        if q == 0:
            gate_up[g, :, span[o]] = total
            gate, up = total[:, : widths[o]], total[:, widths[o] :]
            hidden[g, x, y, :, span1[o]] = (gate * jax.nn.sigmoid(gate) * up).astype(
                jnp.bfloat16
            )
        else:
            gate, up = gate_up[g, :, first], gate_up[g, :, second]
            sigmoid = jax.nn.sigmoid(gate)
            grads[g, x, y, :, first] = (
                total * up * sigmoid * (1.0 + gate * (1.0 - sigmoid))
            ).astype(jnp.bfloat16)
            grads[g, x, y, :, second] = (total * gate * sigmoid).astype(jnp.bfloat16)
        for copy in ag1_copies(q, g, o):
            go(copy)

    def step_g1(q, g, o):
        for copy in ag1_copies(q, g, o):
            copy.wait_recv()
        for copy in ag2_copies(q, g, o)[:4]:
            go(copy)

    def step_g2(q, g, o):
        copies = ag2_copies(q, g, o)
        for side in range(2):
            copies[side].wait_recv()
            go(copies[4 + side])

    depth = down_w.shape[1]
    strip = depth // 2

    def strip_of(c):
        return pl.ds(c * strip, strip)

    def pair_copy(t, g, c):
        return remote(
            acc.at[t, g, :, 1 - k, :, strip_of(c)],
            pair.at[t, g, :, :, strip_of(c)],
            "pair",
            (t, g, c),
            at(dk=1),
        )

    def step_f(q, g):
        for o in range(2):
            for copy in ag2_copies(q, g, o)[2:]:
                copy.wait_recv()
        buf, _ = ag_bufs(q)
        left = buf[g].reshape(NB * HALF, buf.shape[-1])
        for c in range(2):

            @pl.loop(0, strip // TILE)
            def _(n):
                cols = pl.ds(pl.multiple_of(c * strip + n * TILE, TILE), TILE)
                if q == 0:
                    term = jnp.dot(left, down_w[:, cols], preferred_element_type=jnp.float32)
                else:
                    term = lax.dot_general(
                        left, gu_w[cols, :], (((1,), (1,)), ((), ())),
                        preferred_element_type=jnp.float32,
                    )
                acc[q, g, :, :, :, cols] = term.reshape(NZ, 2, HALF, TILE)

            go(pair_copy(q, g, c))

    def z_copy(t, g, c, e):
        j, n, dz, _ = GROUPS[g][e]
        runs = pl.ds(j, n)
        return remote(
            zsend.at[t, g, runs, :, strip_of(c)],
            zrecv.at[t, g, runs, :, strip_of(c)],
            "z",
            (t, g, c, e),
            at(dz=dz),
        )

    def step_z(t, g):
        for c in range(2):
            pair_copy(t, g, c).wait_recv()

            @pl.loop(0, NZ)
            def _(i):
                zsend[t, g, i, :, strip_of(c)] = (
                    acc[t, g, i, k, :, strip_of(c)] + pair[t, g, i, :, strip_of(c)]
                ).astype(jnp.bfloat16)

            for e, (_, _, dz, _) in sorted(
                enumerate(GROUPS[g]), key=lambda run: -abs(run[1][2])
            ):
                if dz:
                    go(z_copy(t, g, c, e))

    def step_out(t, g, last):
        for c in range(2):
            cols = strip_of(c)
            total = [None, None]
            for h in range(2):
                if last:
                    total[h] = result[t, h, :, cols]
                if g == NEAR:
                    own = acc[t, g, 2 + h, k, :, cols] + pair[t, g, 2 + h, :, cols]
                    total[h] = own if total[h] is None else total[h] + own
            for e, (j, n, dz, first) in enumerate(GROUPS[g]):
                if dz:
                    z_copy(t, g, c, e).wait_recv()
                    for i in range(n):
                        h = first + i
                        term = zrecv[t, g, j + i, :, cols].astype(jnp.float32)
                        total[h] = term if total[h] is None else total[h] + term
            for h in range(2):
                if last:
                    both_out[t, h, :, cols] = total[h].astype(jnp.bfloat16)
                else:
                    result[t, h, :, cols] = total[h]

    def both(step, q, g):
        for o in range(2):
            step(q, g, o)

    gather_start(0, NEAR)
    for load in loads[:6]:
        load.start()
    gather_finish(0, NEAR, (0, FAR))
    loads[6].start()
    for load in (loads[0], *loads[2:6]):
        load.wait()
    step_b(0, NEAR)
    both(step_r, 0, NEAR)
    gather_finish(0, FAR, (1, FAR))
    step_b(0, FAR)
    both(step_s1, 0, NEAR)
    both(step_r, 0, FAR)
    gather_finish(1, FAR, (1, NEAR))
    loads[6].wait()
    step_b(1, FAR)
    both(step_s2, 0, NEAR)
    both(step_s1, 0, FAR)
    both(step_r, 1, FAR)
    both(step_g1, 0, NEAR)
    gather_finish(1, NEAR)
    loads[1].wait()
    step_b(1, NEAR)
    both(step_s2, 0, FAR)
    both(step_g2, 0, NEAR)
    both(step_s1, 1, FAR)
    both(step_r, 1, NEAR)
    both(step_g1, 0, FAR)
    both(step_s2, 1, FAR)
    step_f(0, NEAR)
    both(step_g2, 0, FAR)
    both(step_s1, 1, NEAR)
    both(step_g1, 1, FAR)
    step_z(0, NEAR)
    step_f(0, FAR)
    both(step_s2, 1, NEAR)
    both(step_g2, 1, FAR)
    step_z(0, FAR)
    both(step_g1, 1, NEAR)
    step_f(1, FAR)
    step_out(0, NEAR, False)
    both(step_g2, 1, NEAR)
    step_z(1, FAR)
    step_out(0, FAR, True)
    step_f(1, NEAR)
    step_out(1, FAR, False)
    step_z(1, NEAR)
    step_out(1, NEAR, True)
    for copy in pending:
        copy.wait_send()


def finish(both_out, output, input_grad):
    output[...] = both_out[0]
    input_grad[...] = both_out[1]


def body(tokens, cotangent, gate_weight, up_weight, down_weight):
    rows, depth = tokens.shape
    width = gate_weight.shape[1]
    split = (width // 128 + 1) // 2 * 128
    bf16, f32, dma = jnp.bfloat16, jnp.float32, pltpu.SemaphoreType.DMA
    vmem = pltpu.VMEM
    assert rows == 2 * HALF
    scratch = [
        vmem((depth, 2 * width), bf16),
        vmem((width, depth), bf16),
        vmem((2, 2, NZ, 2, HALF, depth), bf16),
        vmem((2, NX, NY, HALF, 2 * width), bf16),
        vmem((2, NX, NY, HALF, width), bf16),
        vmem((2, NX, NY, HALF, 2 * width), f32),
        vmem((2, NX, NY, HALF, width), f32),
        vmem((2, 2, NX, HALF, 2 * width), bf16),
        vmem((2, 2, NX, HALF, width), bf16),
        vmem((2, NX, HALF, 2 * width), bf16),
        vmem((2, NX, HALF, width), bf16),
        vmem((2, NX, HALF, 2 * width), bf16),
        vmem((2, NX, HALF, width), bf16),
        vmem((2, NX - 1, HALF, 2 * width), bf16),
        vmem((2, NX - 1, HALF, width), bf16),
        vmem((2, HALF, 2 * width), f32),
        vmem((2, HALF, width), f32),
        vmem((2, HALF, 2 * width), f32),
        vmem((2, NX, NY, HALF, width), bf16),
        vmem((2, NX, NY, HALF, 2 * width), bf16),
        vmem((2, 2, NZ, 2, HALF, depth), f32),
        vmem((2, 2, NZ, HALF, depth), f32),
        vmem((2, 2, NZ, HALF, depth), bf16),
        vmem((2, 2, NZ, HALF, depth), bf16),
        vmem((2, 2, HALF, depth), f32),
        dma((7,)),
    ]
    scratch += [dma(SEMAPHORES[kind]) for kind in KINDS for _ in range(2)]
    both_out = pl.pallas_call(
        functools.partial(kernel, split),
        name="swiglu_both_ways",
        out_shape=jax.ShapeDtypeStruct((2, 2, HALF, depth), bf16),
        in_specs=[pl.BlockSpec(memory_space=pl.ANY)] * 5,
        out_specs=pl.BlockSpec(memory_space=pltpu.VMEM),
        scratch_shapes=scratch,
        compiler_params=pltpu.CompilerParams(
            collective_id=0, has_side_effects=True, vmem_limit_bytes=60 << 20
        ),
    )(
        tokens.reshape(2, HALF, depth),
        cotangent.reshape(2, HALF, depth),
        gate_weight,
        up_weight,
        down_weight,
    )
    shape = jax.ShapeDtypeStruct((rows, depth), bf16)
    return pl.pallas_call(
        finish,
        name="finish",
        out_shape=(shape, shape),
        in_specs=[pl.BlockSpec(memory_space=pltpu.VMEM)],
        out_specs=(pl.BlockSpec(memory_space=pltpu.VMEM),) * 2,
    )(both_out.reshape(2, rows, depth))


def solution(mesh):
    placed = (P("col", "row"), P("col", "row"), P("row", "col"), P("row", "col"), P("col", "row"))
    return jax.shard_map(
        body,
        mesh=mesh,
        in_specs=placed,
        out_specs=(P("col", "row"), P("col", "row")),
        check_vma=False,
    )
```

```python
import functools

import jax
import jax.numpy as jnp
from jax import lax
from jax.experimental import pallas as pl
from jax.experimental.pallas import tpu as pltpu
from jax.sharding import PartitionSpec as P

MESH = pl.DeviceIdType.MESH
NX, NY, NZ = 4, 4, 8
NB = NX * NY
HALF = 16
TILE = 256
GROUPS = (
    ((0, 2, 0, 0), (2, 2, -1, 0), (4, 2, 1, 0), (6, 1, 2, 0), (7, 1, -2, 0)),
    ((0, 1, 2, 1), (1, 1, -2, 1), (2, 2, 3, 0), (4, 2, -3, 0), (6, 2, 4, 0)),
)
NEAR, FAR = 0, 1
OTHERS = (pl.ds(2, 6), pl.ds(0, 8))
ARRIVALS = {
    "seen": (2, 2),
    "share": (2, 2),
    "relay": (2, 2, 2),
    "rs1": (2, 2, 2),
    "rs2": (2, 2, 2),
    "ag1": (2, 2, 2),
    "first": (2, 2, 2),
    "rest": (2, 2, 2),
    "pair": (2, 2, 2),
    "z": (2, 2, 2),
}
KINDS = tuple(ARRIVALS)
DEPARTURES = {kind: (2, 2) if kind in ("seen", "share", "z") else (2,) for kind in KINDS}
LAST = (0, 0)
STRIPS = ((2, 2), (2, 2))
SCHEDULE = (
    ("gs", 0, 0), ("gs", 0, 1), ("gw", 0, 0), ("gs", 1, 1), ("b", 0, 0, 1), ("b", 0, 0, 0),
    ("b2", 0, 0, 1), ("r", 0, 0, 1), ("b2", 0, 0, 0), ("gw", 0, 1), ("r", 0, 0, 0),
    ("b", 0, 1, 0), ("s1", 0, 0, 1), ("gs", 1, 0), ("b2", 0, 1, 0), ("b", 0, 1, 1),
    ("s1", 0, 0, 0), ("gw", 1, 1), ("b2", 0, 1, 1), ("s2", 0, 0, 1), ("r", 0, 1, 0),
    ("b", 1, 1, 1), ("gw", 1, 0), ("b", 1, 1, 0), ("r", 0, 1, 1), ("b", 1, 0, 0),
    ("s2", 0, 0, 0), ("g1", 0, 0, 1), ("s1", 0, 1, 0), ("b2", 1, 1, 1), ("r", 1, 1, 1),
    ("r", 1, 1, 0), ("b2", 1, 1, 0), ("b", 1, 0, 1), ("g1", 0, 0, 0), ("s1", 0, 1, 1),
    ("b2", 1, 0, 1), ("s2", 0, 1, 0), ("s1", 1, 1, 0), ("b2", 1, 0, 0), ("g2", 0, 0, 1),
    ("r", 1, 0, 0), ("r", 1, 0, 1), ("s1", 1, 1, 1), ("s2", 0, 1, 1), ("g2", 0, 0, 0),
    ("g1", 0, 1, 0), ("s2", 1, 1, 0), ("s2", 1, 1, 1), ("s1", 1, 0, 0), ("g1", 0, 1, 1),
    ("s1", 1, 0, 1), ("f", 0, 0, 1), ("g2", 0, 1, 0), ("g1", 1, 1, 0), ("g2", 0, 1, 1),
    ("g1", 1, 1, 1), ("f", 0, 0, 0), ("z", 0, 0, 1), ("s2", 1, 0, 1), ("s2", 1, 0, 0),
    ("f", 0, 1, 1), ("g2", 1, 1, 0), ("z", 0, 0, 0), ("z", 0, 1, 1), ("g2", 1, 1, 1),
    ("f", 0, 1, 0), ("z", 0, 1, 0), ("g1", 1, 0, 0), ("g1", 1, 0, 1), ("f", 1, 1, 0),
    ("g2", 1, 0, 0), ("g2", 1, 0, 1), ("out", 0, 1, 1), ("z", 1, 1, 0), ("f", 1, 1, 1),
    ("z", 1, 1, 1), ("f", 1, 0, 1), ("f", 1, 0, 0), ("out", 0, 1, 0), ("z", 1, 0, 1),
    ("out", 0, 0, 1), ("z", 1, 0, 0), ("out", 1, 1, 0), ("out", 1, 1, 1), ("out", 0, 0, 0),
    ("out", 1, 0, 1), ("out", 1, 0, 0),
)


def kernel(
    split,
    tokens,
    cotangent,
    gate_weight,
    up_weight,
    down_weight,
    both_out,
    gu_w,
    down_w,
    seen,
    send1_p,
    send1_q,
    full_p,
    full_q,
    recv1_p,
    recv1_q,
    relay_p,
    relay_q,
    send2_p,
    send2_q,
    recv2_p,
    recv2_q,
    own2_p,
    own2_q,
    gate_up,
    hidden,
    grads,
    acc,
    pair,
    zsend,
    zrecv,
    result,
    load_sem,
    *sems,
):
    width = gate_weight.shape[1]
    row, col = lax.axis_index("row"), lax.axis_index("col")
    x, y = row // NY, row % NY
    z, k = col // 2, col % 2

    def at(dx=0, dy=0, dz=0, dk=0):
        return (
            ((x + dx) % NX) * NY + (y + dy) % NY,
            ((z + dz) % NZ) * 2 + (k + dk) % 2,
        )

    def remote(src, dst, kind, index, device):
        send, recv = sems[2 * KINDS.index(kind)], sems[2 * KINDS.index(kind) + 1]
        return pltpu.make_async_remote_copy(
            src_ref=src,
            dst_ref=dst,
            send_sem=send.at[index[: len(DEPARTURES[kind])]],
            recv_sem=recv.at[index],
            device_id=device,
            device_id_type=MESH,
        )

    def arrive(like, kind, index):
        remote(like, like, kind, index, at(dk=1)).wait_recv()

    def depart(like, kind, index):
        index = (*index, 0, 0)[: len(ARRIVALS[kind])]
        remote(like, like, kind, index, at(dk=1)).wait_send()

    offset = (0, split)
    widths = (split, width - split)
    span1 = tuple(pl.ds(offset[o], widths[o]) for o in range(2))
    span2 = tuple(pl.ds(2 * offset[o], 2 * widths[o]) for o in range(2))

    loads = [
        pltpu.make_async_copy(src, dst, load_sem.at[i])
        for i, (src, dst) in enumerate(
            [(tokens, seen.at[0, NEAR, pl.ds(0, 2), k]), (cotangent, seen.at[1, NEAR, pl.ds(0, 2), k])]
            + [
                (
                    src.at[:, span1[o]],
                    gu_w.at[:, pl.ds(2 * offset[o] + p * widths[o], widths[o])],
                )
                for o in range(2)
                for p, src in enumerate((gate_weight, up_weight))
            ]
            + [(down_weight, down_w)]
        )
    ]

    barrier = pltpu.get_barrier_semaphore()
    friends = (
        [at(dx=d) for d in range(1, NX)]
        + [at(dy=d) for d in range(1, NY)]
        + [at(dz=d) for d in range(1, NZ)]
        + [at(dk=1)]
    )
    for friend in friends:
        pl.semaphore_signal(barrier, inc=1, device_id=friend, device_id_type=MESH)
    for load in loads:
        load.start()
    pl.semaphore_wait(barrier, len(friends))

    def go(copy):
        copy.start()

    def own_block(t, n, h):
        return (tokens, cotangent)[t].at[pl.ds(h, n)]

    def step_gs(t, g):
        for j, n, dz, h in GROUPS[g]:
            block = seen.at[t, g, pl.ds(j, n), k]
            if dz:
                go(remote(own_block(t, n, h), block, "seen", (t, g), at(dz=-dz)))
        if g == NEAR:
            own = seen.at[t, g, pl.ds(0, 2), k]
            go(remote(own_block(t, 2, 0), own, "share", (t, g), at(dk=1)))

    def step_gw(t, g):
        block = seen.at[t, g, OTHERS[g], k]
        arrive(block, "seen", (t, g))
        go(remote(block, block, "share", (t, g), at(dk=1)))

    def product(left, weight, turned, full, send, g, start, extent):
        def tile(first, size):
            cols = pl.ds(first, size)
            if turned:
                term = lax.dot_general(
                    left, weight[cols, :], (((1,), (1,)), ((), ())),
                    preferred_element_type=jnp.float32,
                )
            else:
                term = jnp.dot(left, weight[:, cols], preferred_element_type=jnp.float32)
            term = term.reshape(NX, NY, HALF, size)
            full[g, :, :, :, cols] = term
            send[g, :, :, :, cols] = term.astype(jnp.bfloat16)

        count = extent // TILE

        @pl.loop(0, count)
        def _(n):
            tile(pl.multiple_of(start + n * TILE, 128), TILE)

        if extent % TILE:
            tile(start + count * TILE, extent % TILE)

    kinds = (
        (span2, full_p, send1_p, recv1_p, relay_p, send2_p, recv2_p, own2_p),
        (span1, full_q, send1_q, recv1_q, relay_q, send2_q, recv2_q, own2_q),
    )
    low, high, whole = pl.ds(0, NX // 2), pl.ds(NX // 2, NX // 2), pl.ds(0, NX)

    def along_x(g, o):
        return (g + o) % 2 == 0

    def line(g, o, step):
        if along_x(g, o):
            return at(dx=step), (x + step) % NX
        return at(dy=step), (y + step) % NY

    def cross(g, o, step):
        return line(g + 1, o, step)

    def part(buf, g, o, chunk, inner, cols):
        if along_x(g, o):
            return buf.at[g, chunk, inner, :, cols]
        return buf.at[g, inner, chunk, :, cols]

    def rs1_copies(q, g, o):
        span, _, send1, recv1, relay, _, _, _ = kinds[q]
        (right, after), (left, before) = line(g, o, 1), line(g, o, -1)
        _, opposite = line(g, o, 2)
        plan = [
            ("relay", right, opposite, low, relay.at[g, low, :, span[o]]),
            ("relay", left, opposite, high, relay.at[g, high, :, span[o]]),
            ("rs1", right, after, high, recv1.at[g, 0, high, :, span[o]]),
            ("rs1", left, before, low, recv1.at[g, 1, low, :, span[o]]),
            ("rs1", right, after, low, recv1.at[g, 0, low, :, span[o]]),
            ("rs1", left, before, high, recv1.at[g, 1, high, :, span[o]]),
        ]
        return [
            remote(part(send1, g, o, chunk, inner, span[o]), dst, kind, (q, g, o), device)
            for kind, device, chunk, inner, dst in plan
        ]

    arrived = set()

    def once(key, wait):
        if key not in arrived:
            arrived.add(key)
            wait()

    def tokens_there(q, g):
        arrive(seen.at[q, g, :, k], "share", (q, g))
        if g == NEAR:
            loads[q].wait()

    def step_b(q, g, o):
        once(("seen", q, g), lambda: tokens_there(q, g))
        for n in (6,) if q else (2, 3, 4, 5):
            once(("load", n), loads[n].wait)
        left = seen[q, g].reshape(NB * HALF, seen.shape[-1])
        if q == 0:
            product(left, gu_w, False, full_p, send1_p, g, 2 * offset[o], 2 * widths[o])
        else:
            product(left, down_w, True, full_q, send1_q, g, offset[o], widths[o])
        for copy in rs1_copies(q, g, o)[:2]:
            go(copy)

    def step_b2(q, g, o):
        for copy in rs1_copies(q, g, o)[2:4]:
            go(copy)

    def step_r(q, g, o):
        span, full, send1, _, relay, _, _, _ = kinds[q]
        copies = rs1_copies(q, g, o)
        arrive(relay.at[g, :, :, span[o]], "relay", (q, g, o))
        for side, blocks in enumerate((range(NX // 2), range(NX // 2, NX))):
            _, chunk = line(g, o, 1 - 2 * side)
            for i in blocks:
                total = part(full, g, o, chunk, i, span[o])[...]
                total += relay[g, i, :, span[o]].astype(jnp.float32)
                part(send1, g, o, chunk, i, span[o])[...] = total.astype(jnp.bfloat16)
            go(copies[side - 2])

    def rs2_copies(q, g, o):
        span, _, _, _, _, send2, recv2, _ = kinds[q]
        return [
            remote(
                send2.at[g, cross(g, o, d)[1], :, span[o]],
                recv2.at[g, d - 1, :, span[o]],
                "rs2",
                (q, g, o),
                cross(g, o, d)[0],
            )
            for d in range(1, NX)
        ]

    def step_s1(q, g, o):
        span, full, _, recv1, _, send2, _, own2 = kinds[q]
        arrive(recv1.at[g, :, :, :, span[o]], "rs1", (q, g, o))

        def total(i):
            mine = part(full, g, o, line(g, o, 0)[1], i, span[o])[...]
            for d in range(2):
                mine += recv1[g, d, i, :, span[o]].astype(jnp.float32)
            return mine

        for i in range(NX):
            send2[g, i, :, span[o]] = total(i).astype(jnp.bfloat16)
        own2[g, :, span[o]] = total(cross(g, o, 0)[1])
        for copy in rs2_copies(q, g, o):
            go(copy)

    def ag_bufs(q):
        return (hidden, span1) if q == 0 else (grads, span2)

    def ag1_copies(q, g, o):
        buf, span = ag_bufs(q)
        mine = buf.at[g, x, y, :, span[o]]
        return [
            remote(
                mine,
                mine,
                "ag1",
                (q, g, o),
                cross(g, o, d)[0],
            )
            for d in range(1, NX)
        ]

    def ag2_copies(q, g, o):
        buf, span = ag_bufs(q)
        (right, after), (left, before) = line(g, o, 1), line(g, o, -1)
        _, mine = line(g, o, 0)
        plan = [
            ("first", right, mine, low),
            ("first", left, mine, high),
            ("rest", right, mine, high),
            ("rest", left, mine, low),
            ("rest", right, before, low),
            ("rest", left, after, high),
        ]
        return [
            remote(
                part(buf, g, o, chunk, inner, span[o]),
                part(buf, g, o, chunk, inner, span[o]),
                kind,
                (q, g, o),
                device,
            )
            for kind, device, chunk, inner in plan
        ]

    def step_s2(q, g, o):
        span, _, _, _, _, _, recv2, own2 = kinds[q]
        arrive(recv2.at[g, :, :, span[o]], "rs2", (q, g, o))
        total = own2[g, :, span[o]]
        for d in range(NX - 1):
            total += recv2[g, d, :, span[o]].astype(jnp.float32)
        first, second = (
            pl.ds(2 * offset[o], widths[o]),
            pl.ds(2 * offset[o] + widths[o], widths[o]),
        )
        if q == 0:
            gate_up[g, :, span[o]] = total
            gate, up = total[:, : widths[o]], total[:, widths[o] :]
            hidden[g, x, y, :, span1[o]] = (gate * jax.nn.sigmoid(gate) * up).astype(
                jnp.bfloat16
            )
        else:
            gate, up = gate_up[g, :, first], gate_up[g, :, second]
            sigmoid = jax.nn.sigmoid(gate)
            grads[g, x, y, :, first] = (
                total * up * sigmoid * (1.0 + gate * (1.0 - sigmoid))
            ).astype(jnp.bfloat16)
            grads[g, x, y, :, second] = (total * gate * sigmoid).astype(jnp.bfloat16)
        for copy in ag1_copies(q, g, o):
            go(copy)

    def step_g1(q, g, o):
        buf, span = ag_bufs(q)
        arrive(buf.at[g, 0, pl.ds(0, NX - 1), :, span[o]], "ag1", (q, g, o))
        for copy in ag2_copies(q, g, o)[:4]:
            go(copy)

    def step_g2(q, g, o):
        buf, span = ag_bufs(q)
        arrive(buf.at[g, 0, :, :, span[o]], "first", (q, g, o))
        for copy in ag2_copies(q, g, o)[4:]:
            go(copy)

    depth = down_w.shape[1]

    def strip_of(q, g, c):
        size = depth // STRIPS[q][g]
        return pl.ds(c * size, size)

    def pair_copy(t, g, c):
        return remote(
            acc.at[t, g, :, 1 - k, :, strip_of(t, g, c)],
            pair.at[t, g, :, :, strip_of(t, g, c)],
            "pair",
            (t, g, c),
            at(dk=1),
        )

    def rows_there(q, g):
        buf, span = ag_bufs(q)
        for o in range(2):
            arrive(buf.at[g, pl.ds(0, 2), :, :, span[o]], "rest", (q, g, o))

    def step_f(q, g, c):
        once(("rows", q, g), lambda: rows_there(q, g))
        buf, _ = ag_bufs(q)
        left = buf[g].reshape(NB * HALF, buf.shape[-1])

        strip = strip_of(q, g, c)

        @pl.loop(0, strip.size // TILE)
        def _(n):
            cols = pl.ds(pl.multiple_of(strip.start + n * TILE, TILE), TILE)
            if q == 0:
                term = jnp.dot(left, down_w[:, cols], preferred_element_type=jnp.float32)
            else:
                term = lax.dot_general(
                    left, gu_w[cols, :], (((1,), (1,)), ((), ())),
                    preferred_element_type=jnp.float32,
                )
            acc[q, g, :, :, :, cols] = term.reshape(NZ, 2, HALF, TILE)

        go(pair_copy(q, g, c))

    def z_copy(t, g, c, e):
        j, n, dz, _ = GROUPS[g][e]
        runs = pl.ds(j, n)
        return remote(
            zsend.at[t, g, runs, :, strip_of(t, g, c)],
            zrecv.at[t, g, runs, :, strip_of(t, g, c)],
            "z",
            (t, g, c),
            at(dz=dz),
        )

    def step_z(t, g, c):
        pair_copy(t, g, c).wait_recv()

        @pl.loop(0, NZ)
        def _(i):
            zsend[t, g, i, :, strip_of(t, g, c)] = (
                acc[t, g, i, k, :, strip_of(t, g, c)] + pair[t, g, i, :, strip_of(t, g, c)]
            ).astype(jnp.bfloat16)

        for e, (_, _, dz, _) in sorted(enumerate(GROUPS[g]), key=lambda run: -abs(run[1][2])):
            if dz:
                go(z_copy(t, g, c, e))

    def step_out(t, g, c):
        cols = strip_of(t, g, c)
        last = g == LAST[t]
        total = [result[t, h, :, cols] if last else None for h in range(2)]
        if g == NEAR:
            for h in range(2):
                own = acc[t, g, h, k, :, cols] + pair[t, g, h, :, cols]
                total[h] = own if total[h] is None else total[h] + own
        arrive(zrecv.at[t, g, OTHERS[g], :, cols], "z", (t, g, c))
        for j, n, dz, first in GROUPS[g]:
            if dz:
                for i in range(n):
                    h = first + i
                    term = zrecv[t, g, j + i, :, cols].astype(jnp.float32)
                    total[h] = term if total[h] is None else total[h] + term
        for h in range(2):
            if last:
                both_out[t, h, :, cols] = total[h].astype(jnp.bfloat16)
            else:
                result[t, h, :, cols] = total[h]

    steps = {
        "gs": step_gs,
        "gw": step_gw,
        "b": step_b,
        "b2": step_b2,
        "r": step_r,
        "s1": step_s1,
        "s2": step_s2,
        "g1": step_g1,
        "g2": step_g2,
        "f": step_f,
        "z": step_z,
        "out": step_out,
    }
    for step, *where in SCHEDULE:
        steps[step](*where)

    for q in range(2):
        _, _, _, recv1, relay, _, recv2, _ = kinds[q]
        buf, _ = ag_bufs(q)
        for g in range(2):
            depart(seen.at[q, g, OTHERS[g], k], "seen", (q, g))
            depart(seen.at[q, g, :, k], "share", (q, g))
            depart(zrecv.at[q, g, OTHERS[g]], "z", (q, g))
        depart(relay, "relay", (q,))
        depart(recv1, "rs1", (q,))
        depart(recv2, "rs2", (q,))
        depart(buf.at[:, 0, pl.ds(0, NX - 1)], "ag1", (q,))
        depart(buf.at[:, 0], "first", (q,))
        depart(buf.at[:, pl.ds(0, 2)], "rest", (q,))
        depart(pair.at[q], "pair", (q,))


def finish(both_out, output, input_grad):
    output[...] = both_out[0]
    input_grad[...] = both_out[1]


def body(tokens, cotangent, gate_weight, up_weight, down_weight):
    rows, depth = tokens.shape
    width = gate_weight.shape[1]
    split = (width // 128 + 1) // 2 * 128
    bf16, f32, dma = jnp.bfloat16, jnp.float32, pltpu.SemaphoreType.DMA
    vmem = pltpu.VMEM
    assert rows == 2 * HALF
    scratch = [
        vmem((depth, 2 * width), bf16),
        vmem((width, depth), bf16),
        vmem((2, 2, NZ, 2, HALF, depth), bf16),
        vmem((2, NX, NY, HALF, 2 * width), bf16),
        vmem((2, NX, NY, HALF, width), bf16),
        vmem((2, NX, NY, HALF, 2 * width), f32),
        vmem((2, NX, NY, HALF, width), f32),
        vmem((2, 2, NX, HALF, 2 * width), bf16),
        vmem((2, 2, NX, HALF, width), bf16),
        vmem((2, NX, HALF, 2 * width), bf16),
        vmem((2, NX, HALF, width), bf16),
        vmem((2, NX, HALF, 2 * width), bf16),
        vmem((2, NX, HALF, width), bf16),
        vmem((2, NX - 1, HALF, 2 * width), bf16),
        vmem((2, NX - 1, HALF, width), bf16),
        vmem((2, HALF, 2 * width), f32),
        vmem((2, HALF, width), f32),
        vmem((2, HALF, 2 * width), f32),
        vmem((2, NX, NY, HALF, width), bf16),
        vmem((2, NX, NY, HALF, 2 * width), bf16),
        vmem((2, 2, NZ, 2, HALF, depth), f32),
        vmem((2, 2, NZ, HALF, depth), f32),
        vmem((2, 2, NZ, HALF, depth), bf16),
        vmem((2, 2, NZ, HALF, depth), bf16),
        vmem((2, 2, HALF, depth), f32),
        dma((7,)),
    ]
    scratch += [dma(shapes[kind]) for kind in KINDS for shapes in (DEPARTURES, ARRIVALS)]
    both_out = pl.pallas_call(
        functools.partial(kernel, split),
        name="swiglu_both_ways",
        out_shape=jax.ShapeDtypeStruct((2, 2, HALF, depth), bf16),
        in_specs=[pl.BlockSpec(memory_space=pl.ANY)] * 5,
        out_specs=pl.BlockSpec(memory_space=pltpu.VMEM),
        scratch_shapes=scratch,
        compiler_params=pltpu.CompilerParams(
            collective_id=0, has_side_effects=True, vmem_limit_bytes=60 << 20
        ),
    )(
        tokens.reshape(2, HALF, depth),
        cotangent.reshape(2, HALF, depth),
        gate_weight,
        up_weight,
        down_weight,
    )
    shape = jax.ShapeDtypeStruct((rows, depth), bf16)
    return pl.pallas_call(
        finish,
        name="finish",
        out_shape=(shape, shape),
        in_specs=[pl.BlockSpec(memory_space=pltpu.VMEM)],
        out_specs=(pl.BlockSpec(memory_space=pltpu.VMEM),) * 2,
    )(both_out.reshape(2, rows, depth))


def solution(mesh):
    placed = (P("col", "row"), P("col", "row"), P("row", "col"), P("row", "col"), P("col", "row"))
    return jax.shard_map(
        body,
        mesh=mesh,
        in_specs=placed,
        out_specs=(P("col", "row"), P("col", "row")),
        check_vma=False,
    )
```

```python
import functools

import jax
import jax.numpy as jnp
from jax import lax
from jax.experimental import pallas as pl
from jax.experimental.pallas import tpu as pltpu
from jax.sharding import PartitionSpec as P

MESH = pl.DeviceIdType.MESH
NX, NY, NZ = 4, 4, 8
NB = NX * NY
HALF = 16
TILE = 256
GROUPS = (
    ((0, 2, 0, 0), (2, 2, -1, 0), (4, 2, 1, 0), (6, 1, 2, 0), (7, 1, -2, 0)),
    ((0, 1, 2, 1), (1, 1, -2, 1), (2, 2, 3, 0), (4, 2, -3, 0), (6, 2, 4, 0)),
)
NEAR, FAR = 0, 1
OTHERS = (pl.ds(2, 6), pl.ds(0, 8))
ARRIVALS = {
    "seen": (2, 2),
    "share": (2, 2),
    "relay": (2, 2, 2),
    "rs1": (2, 2, 2),
    "rs2": (2, 2, 2),
    "ag1": (2, 2, 2),
    "ag1on": (2, 2, 2),
    "first": (2, 2, 2),
    "rest": (2, 2, 2),
    "pair": (2, 2, 2),
    "z": (2, 2, 2),
}
KINDS = tuple(ARRIVALS)
DEPARTURES = {kind: (2, 2) if kind in ("seen", "share", "z") else (2,) for kind in KINDS}
LAST = (0, 0)
STRIPS = ((2, 2), (2, 2))
SCHEDULE = (
    ("gs", 0, 0), ("gs", 0, 1), ("gw", 0, 0), ("b", 0, 0, 0), ("b", 0, 0, 1), ("gs", 1, 1),
    ("b2", 0, 0, 0), ("b2", 0, 0, 1), ("gw", 0, 1), ("r", 0, 0, 0), ("r", 0, 0, 1),
    ("b", 0, 1, 0), ("b2", 0, 1, 0), ("b", 0, 1, 1), ("gs", 1, 0), ("s1", 0, 0, 0),
    ("s1", 0, 0, 1), ("b2", 0, 1, 1), ("r", 0, 1, 0), ("gw", 1, 1), ("r", 0, 1, 1),
    ("s2", 0, 0, 1), ("gw", 1, 0), ("b", 1, 1, 0), ("b", 1, 1, 1), ("b2", 1, 1, 1),
    ("b", 1, 0, 1), ("b2", 1, 1, 0), ("s2", 0, 0, 0), ("b", 1, 0, 0), ("g0", 0, 0, 1),
    ("s1", 0, 1, 0), ("r", 1, 1, 0), ("r", 1, 1, 1), ("s1", 0, 1, 1), ("r", 1, 0, 0),
    ("b2", 1, 0, 0), ("g0", 0, 0, 0), ("b2", 1, 0, 1), ("s2", 0, 1, 0), ("s1", 1, 1, 0),
    ("r", 1, 0, 1), ("s2", 0, 1, 1), ("g1", 0, 0, 0), ("s1", 1, 1, 1), ("g1", 0, 0, 1),
    ("g0", 0, 1, 0), ("s1", 1, 0, 1), ("g0", 0, 1, 1), ("s1", 1, 0, 0), ("s2", 1, 1, 0),
    ("s2", 1, 1, 1), ("g2", 0, 0, 1), ("g2", 0, 0, 0), ("g1", 0, 1, 0), ("g1", 0, 1, 1),
    ("g0", 1, 1, 0), ("g0", 1, 1, 1), ("s2", 1, 0, 0), ("f", 0, 0, 1, 1), ("f", 0, 0, 1, 0),
    ("p", 0, 0, 1), ("g2", 0, 1, 1), ("g2", 0, 1, 0), ("f", 0, 0, 0, 1), ("s2", 1, 0, 1),
    ("f", 0, 0, 0, 0), ("z", 0, 0, 1), ("p", 0, 0, 0), ("g1", 1, 1, 0), ("g1", 1, 1, 1),
    ("f", 0, 1, 1, 1), ("f", 0, 1, 1, 0), ("p", 0, 1, 1), ("f", 0, 1, 0, 1), ("z", 0, 0, 0),
    ("g0", 1, 0, 1), ("f", 0, 1, 0, 0), ("g0", 1, 0, 0), ("z", 0, 1, 1), ("p", 0, 1, 0),
    ("g2", 1, 1, 1), ("g2", 1, 1, 0), ("g1", 1, 0, 1), ("g1", 1, 0, 0), ("z", 0, 1, 0),
    ("f", 1, 1, 1, 1), ("f", 1, 1, 1, 0), ("p", 1, 1, 1), ("f", 1, 1, 0, 0), ("f", 1, 1, 0, 1),
    ("g2", 1, 0, 1), ("z", 1, 1, 1), ("out", 0, 1, 1), ("g2", 1, 0, 0), ("p", 1, 1, 0),
    ("out", 0, 1, 0), ("z", 1, 1, 0), ("f", 1, 0, 0, 1), ("f", 1, 0, 1, 1), ("f", 1, 0, 1, 0),
    ("out", 0, 0, 0), ("p", 1, 0, 1), ("out", 0, 0, 1), ("f", 1, 0, 0, 0), ("p", 1, 0, 0),
    ("z", 1, 0, 1), ("z", 1, 0, 0), ("out", 1, 1, 1), ("out", 1, 1, 0), ("out", 1, 0, 1),
    ("out", 1, 0, 0),
)


def kernel(
    split,
    tokens,
    cotangent,
    gate_weight,
    up_weight,
    down_weight,
    both_out,
    gu_w,
    down_w,
    seen,
    send1_p,
    send1_q,
    full_p,
    full_q,
    recv1_p,
    recv1_q,
    relay_p,
    relay_q,
    send2_p,
    send2_q,
    recv2_p,
    recv2_q,
    own2_p,
    own2_q,
    gate_up,
    hidden,
    grads,
    acc,
    pair,
    zsend,
    zrecv,
    result,
    load_sem,
    *sems,
):
    width = gate_weight.shape[1]
    row, col = lax.axis_index("row"), lax.axis_index("col")
    x, y = row // NY, row % NY
    z, k = col // 2, col % 2

    def at(dx=0, dy=0, dz=0, dk=0):
        return (
            ((x + dx) % NX) * NY + (y + dy) % NY,
            ((z + dz) % NZ) * 2 + (k + dk) % 2,
        )

    def remote(src, dst, kind, index, device):
        send, recv = sems[2 * KINDS.index(kind)], sems[2 * KINDS.index(kind) + 1]
        return pltpu.make_async_remote_copy(
            src_ref=src,
            dst_ref=dst,
            send_sem=send.at[index[: len(DEPARTURES[kind])]],
            recv_sem=recv.at[index],
            device_id=device,
            device_id_type=MESH,
        )

    def arrive(like, kind, index):
        remote(like, like, kind, index, at(dk=1)).wait_recv()

    def depart(like, kind, index):
        index = (*index, 0, 0)[: len(ARRIVALS[kind])]
        remote(like, like, kind, index, at(dk=1)).wait_send()

    offset = (0, split)
    widths = (split, width - split)
    span1 = tuple(pl.ds(offset[o], widths[o]) for o in range(2))
    span2 = tuple(pl.ds(2 * offset[o], 2 * widths[o]) for o in range(2))

    loads = [
        pltpu.make_async_copy(src, dst, load_sem.at[i])
        for i, (src, dst) in enumerate(
            [(tokens, seen.at[0, NEAR, pl.ds(0, 2), k]), (cotangent, seen.at[1, NEAR, pl.ds(0, 2), k])]
            + [
                (
                    src.at[:, span1[o]],
                    gu_w.at[:, pl.ds(2 * offset[o] + p * widths[o], widths[o])],
                )
                for o in range(2)
                for p, src in enumerate((gate_weight, up_weight))
            ]
            + [(down_weight, down_w)]
        )
    ]

    barrier = pltpu.get_barrier_semaphore()
    friends = (
        [at(dx=d) for d in range(1, NX)]
        + [at(dy=d) for d in range(1, NY)]
        + [at(dz=d) for d in range(1, NZ)]
        + [at(dk=1)]
    )
    for friend in friends:
        pl.semaphore_signal(barrier, inc=1, device_id=friend, device_id_type=MESH)
    for load in loads:
        load.start()
    pl.semaphore_wait(barrier, len(friends))

    def go(copy):
        copy.start()

    def own_block(t, n, h):
        return (tokens, cotangent)[t].at[pl.ds(h, n)]

    def step_gs(t, g):
        for j, n, dz, h in GROUPS[g]:
            block = seen.at[t, g, pl.ds(j, n), k]
            if dz:
                go(remote(own_block(t, n, h), block, "seen", (t, g), at(dz=-dz)))
        if g == NEAR:
            own = seen.at[t, g, pl.ds(0, 2), k]
            go(remote(own_block(t, 2, 0), own, "share", (t, g), at(dk=1)))

    def step_gw(t, g):
        block = seen.at[t, g, OTHERS[g], k]
        arrive(block, "seen", (t, g))
        go(remote(block, block, "share", (t, g), at(dk=1)))

    def product(left, weight, turned, full, send, g, start, extent):
        def tile(first, size):
            cols = pl.ds(first, size)
            if turned:
                term = lax.dot_general(
                    left, weight[cols, :], (((1,), (1,)), ((), ())),
                    preferred_element_type=jnp.float32,
                )
            else:
                term = jnp.dot(left, weight[:, cols], preferred_element_type=jnp.float32)
            term = term.reshape(NX, NY, HALF, size)
            full[g, :, :, :, cols] = term
            send[g, :, :, :, cols] = term.astype(jnp.bfloat16)

        for first in range(start, start + extent, TILE):
            tile(first, min(TILE, start + extent - first))

    kinds = (
        (span2, full_p, send1_p, recv1_p, relay_p, send2_p, recv2_p, own2_p),
        (span1, full_q, send1_q, recv1_q, relay_q, send2_q, recv2_q, own2_q),
    )
    low, high, whole = pl.ds(0, NX // 2), pl.ds(NX // 2, NX // 2), pl.ds(0, NX)

    def along_x(g, o):
        return (g + o) % 2 == 0

    def line(g, o, step):
        if along_x(g, o):
            return at(dx=step), (x + step) % NX
        return at(dy=step), (y + step) % NY

    def cross(g, o, step):
        return line(g + 1, o, step)

    def part(buf, g, o, chunk, inner, cols):
        if along_x(g, o):
            return buf.at[g, chunk, inner, :, cols]
        return buf.at[g, inner, chunk, :, cols]

    def rs1_copies(q, g, o):
        span, _, send1, recv1, relay, _, _, _ = kinds[q]
        (right, after), (left, before) = line(g, o, 1), line(g, o, -1)
        _, opposite = line(g, o, 2)
        plan = [
            ("relay", right, opposite, low, relay.at[g, low, :, span[o]]),
            ("relay", left, opposite, high, relay.at[g, high, :, span[o]]),
            ("rs1", right, after, high, recv1.at[g, 0, high, :, span[o]]),
            ("rs1", left, before, low, recv1.at[g, 1, low, :, span[o]]),
            ("rs1", right, after, low, recv1.at[g, 0, low, :, span[o]]),
            ("rs1", left, before, high, recv1.at[g, 1, high, :, span[o]]),
        ]
        return [
            remote(part(send1, g, o, chunk, inner, span[o]), dst, kind, (q, g, o), device)
            for kind, device, chunk, inner, dst in plan
        ]

    arrived = set()

    def once(key, wait):
        if key not in arrived:
            arrived.add(key)
            wait()

    def tokens_there(q, g):
        arrive(seen.at[q, g, :, k], "share", (q, g))
        if g == NEAR:
            loads[q].wait()

    def step_b(q, g, o):
        once(("seen", q, g), lambda: tokens_there(q, g))
        for n in (6,) if q else (2, 3, 4, 5):
            once(("load", n), loads[n].wait)
        left = seen[q, g].reshape(NB * HALF, seen.shape[-1])
        if q == 0:
            product(left, gu_w, False, full_p, send1_p, g, 2 * offset[o], 2 * widths[o])
        else:
            product(left, down_w, True, full_q, send1_q, g, offset[o], widths[o])
        for copy in rs1_copies(q, g, o)[:2]:
            go(copy)

    def step_b2(q, g, o):
        for copy in rs1_copies(q, g, o)[2:4]:
            go(copy)

    def step_r(q, g, o):
        span, full, send1, _, relay, _, _, _ = kinds[q]
        copies = rs1_copies(q, g, o)
        arrive(relay.at[g, :, :, span[o]], "relay", (q, g, o))
        for side, blocks in enumerate((range(NX // 2), range(NX // 2, NX))):
            _, chunk = line(g, o, 1 - 2 * side)
            for i in blocks:
                total = part(full, g, o, chunk, i, span[o])[...]
                total += relay[g, i, :, span[o]].astype(jnp.float32)
                part(send1, g, o, chunk, i, span[o])[...] = total.astype(jnp.bfloat16)
            go(copies[side - 2])

    def rs2_copies(q, g, o):
        span, _, _, _, _, send2, recv2, _ = kinds[q]
        return [
            remote(
                send2.at[g, cross(g, o, d)[1], :, span[o]],
                recv2.at[g, d - 1, :, span[o]],
                "rs2",
                (q, g, o),
                cross(g, o, d)[0],
            )
            for d in range(1, NX)
        ]

    def step_s1(q, g, o):
        span, full, _, recv1, _, send2, _, own2 = kinds[q]
        arrive(recv1.at[g, :, :, :, span[o]], "rs1", (q, g, o))

        def total(i):
            mine = part(full, g, o, line(g, o, 0)[1], i, span[o])[...]
            for d in range(2):
                mine += recv1[g, d, i, :, span[o]].astype(jnp.float32)
            return mine

        for i in range(NX):
            send2[g, i, :, span[o]] = total(i).astype(jnp.bfloat16)
        own2[g, :, span[o]] = total(cross(g, o, 0)[1])
        for copy in rs2_copies(q, g, o):
            go(copy)

    def ag_bufs(q):
        return (hidden, span1) if q == 0 else (grads, span2)

    def spot(g, o, step):
        device, place = cross(g, o, step)
        return device, (x, place) if along_x(g, o) else (place, y)

    def ag1_start(q, g, o):
        buf, span = ag_bufs(q)
        mine = buf.at[g, x, y, :, span[o]]
        for step in (1, -1):
            go(remote(mine, mine, "ag1", (q, g, o), spot(g, o, step)[0]))

    def step_g0(q, g, o):
        buf, span = ag_bufs(q)
        arrive(buf.at[g, 0, pl.ds(0, 2), :, span[o]], "ag1", (q, g, o))
        head = (span[o].size // 128 + 1) // 2 * 128
        for step, start, size in ((1, 0, head), (-1, head, span[o].size - head)):
            block = buf.at[(g, *spot(g, o, -step)[1], slice(None), pl.ds(span[o].start + start, size))]
            go(remote(block, block, "ag1on", (q, g, o), spot(g, o, step)[0]))

    def ag2_copies(q, g, o):
        buf, span = ag_bufs(q)
        (right, after), (left, before) = line(g, o, 1), line(g, o, -1)
        _, mine = line(g, o, 0)
        plan = [
            ("first", right, mine, low),
            ("first", left, mine, high),
            ("rest", right, mine, high),
            ("rest", left, mine, low),
            ("rest", right, before, low),
            ("rest", left, after, high),
        ]
        return [
            remote(
                part(buf, g, o, chunk, inner, span[o]),
                part(buf, g, o, chunk, inner, span[o]),
                kind,
                (q, g, o),
                device,
            )
            for kind, device, chunk, inner in plan
        ]

    def step_s2(q, g, o):
        span, _, _, _, _, _, recv2, own2 = kinds[q]
        arrive(recv2.at[g, :, :, span[o]], "rs2", (q, g, o))
        total = own2[g, :, span[o]]
        for d in range(NX - 1):
            total += recv2[g, d, :, span[o]].astype(jnp.float32)
        first, second = (
            pl.ds(2 * offset[o], widths[o]),
            pl.ds(2 * offset[o] + widths[o], widths[o]),
        )
        if q == 0:
            gate_up[g, :, span[o]] = total
            gate, up = total[:, : widths[o]], total[:, widths[o] :]
            hidden[g, x, y, :, span1[o]] = (gate * jax.nn.sigmoid(gate) * up).astype(
                jnp.bfloat16
            )
        else:
            gate, up = gate_up[g, :, first], gate_up[g, :, second]
            sigmoid = jax.nn.sigmoid(gate)
            grads[g, x, y, :, first] = (
                total * up * sigmoid * (1.0 + gate * (1.0 - sigmoid))
            ).astype(jnp.bfloat16)
            grads[g, x, y, :, second] = (total * gate * sigmoid).astype(jnp.bfloat16)
        ag1_start(q, g, o)

    def step_g1(q, g, o):
        buf, span = ag_bufs(q)
        arrive(buf.at[g, 0, 0, :, span[o]], "ag1on", (q, g, o))
        for copy in ag2_copies(q, g, o)[:4]:
            go(copy)

    def step_g2(q, g, o):
        buf, span = ag_bufs(q)
        arrive(buf.at[g, 0, :, :, span[o]], "first", (q, g, o))
        for copy in ag2_copies(q, g, o)[4:]:
            go(copy)

    depth = down_w.shape[1]

    def strip_of(q, g, c):
        size = depth // STRIPS[q][g]
        return pl.ds(c * size, size)

    def pair_copy(t, g, c):
        return remote(
            acc.at[t, g, :, 1 - k, :, strip_of(t, g, c)],
            pair.at[t, g, :, :, strip_of(t, g, c)],
            "pair",
            (t, g, c),
            at(dk=1),
        )

    def step_f(q, g, c, o):
        buf, span = ag_bufs(q)
        once(
            ("rows", q, g, o),
            lambda: arrive(buf.at[g, pl.ds(0, 2), :, :, span[o]], "rest", (q, g, o)),
        )
        left = buf[g, :, :, :, span[o]].reshape(NB * HALF, span[o].size)
        strip = strip_of(q, g, c)
        more = ("part", q, g, c) in arrived
        arrived.add(("part", q, g, c))
        for n in range(strip.size // TILE):
            cols = pl.ds(strip.start + n * TILE, TILE)
            if q == 0:
                term = jnp.dot(left, down_w[span[o], cols], preferred_element_type=jnp.float32)
            else:
                term = lax.dot_general(
                    left, gu_w[cols, span[o]], (((1,), (1,)), ((), ())),
                    preferred_element_type=jnp.float32,
                )
            term = term.reshape(NZ, 2, HALF, TILE)
            acc[q, g, :, :, :, cols] = acc[q, g, :, :, :, cols] + term if more else term

    def step_p(q, g, c):
        go(pair_copy(q, g, c))

    def z_copy(t, g, c, e):
        j, n, dz, _ = GROUPS[g][e]
        runs = pl.ds(j, n)
        return remote(
            zsend.at[t, g, runs, :, strip_of(t, g, c)],
            zrecv.at[t, g, runs, :, strip_of(t, g, c)],
            "z",
            (t, g, c),
            at(dz=dz),
        )

    def step_z(t, g, c):
        pair_copy(t, g, c).wait_recv()

        @pl.loop(0, NZ)
        def _(i):
            zsend[t, g, i, :, strip_of(t, g, c)] = (
                acc[t, g, i, k, :, strip_of(t, g, c)] + pair[t, g, i, :, strip_of(t, g, c)]
            ).astype(jnp.bfloat16)

        for e, (_, _, dz, _) in sorted(enumerate(GROUPS[g]), key=lambda run: -abs(run[1][2])):
            if dz:
                go(z_copy(t, g, c, e))

    def step_out(t, g, c):
        cols = strip_of(t, g, c)
        last = g == LAST[t]
        total = [result[t, h, :, cols] if last else None for h in range(2)]
        if g == NEAR:
            for h in range(2):
                own = acc[t, g, h, k, :, cols] + pair[t, g, h, :, cols]
                total[h] = own if total[h] is None else total[h] + own
        arrive(zrecv.at[t, g, OTHERS[g], :, cols], "z", (t, g, c))
        for j, n, dz, first in GROUPS[g]:
            if dz:
                for i in range(n):
                    h = first + i
                    term = zrecv[t, g, j + i, :, cols].astype(jnp.float32)
                    total[h] = term if total[h] is None else total[h] + term
        for h in range(2):
            if last:
                both_out[t, h, :, cols] = total[h].astype(jnp.bfloat16)
            else:
                result[t, h, :, cols] = total[h]

    steps = {
        "gs": step_gs,
        "gw": step_gw,
        "b": step_b,
        "b2": step_b2,
        "r": step_r,
        "s1": step_s1,
        "s2": step_s2,
        "g0": step_g0,
        "g1": step_g1,
        "p": step_p,
        "g2": step_g2,
        "f": step_f,
        "z": step_z,
        "out": step_out,
    }
    for step, *where in SCHEDULE:
        steps[step](*where)

    for q in range(2):
        _, _, _, recv1, relay, _, recv2, _ = kinds[q]
        buf, _ = ag_bufs(q)
        for g in range(2):
            depart(seen.at[q, g, OTHERS[g], k], "seen", (q, g))
            depart(seen.at[q, g, :, k], "share", (q, g))
            depart(zrecv.at[q, g, OTHERS[g]], "z", (q, g))
        depart(relay, "relay", (q,))
        depart(recv1, "rs1", (q,))
        depart(recv2, "rs2", (q,))
        depart(buf.at[:, 0, pl.ds(0, 2)], "ag1", (q,))
        depart(buf.at[:, 0, 0], "ag1on", (q,))
        depart(buf.at[:, 0], "first", (q,))
        depart(buf.at[:, pl.ds(0, 2)], "rest", (q,))
        depart(pair.at[q], "pair", (q,))


def finish(both_out, output, input_grad):
    output[...] = both_out[0]
    input_grad[...] = both_out[1]


def body(tokens, cotangent, gate_weight, up_weight, down_weight):
    rows, depth = tokens.shape
    width = gate_weight.shape[1]
    split = (width // 128 + 1) // 2 * 128
    bf16, f32, dma = jnp.bfloat16, jnp.float32, pltpu.SemaphoreType.DMA
    vmem = pltpu.VMEM
    assert rows == 2 * HALF
    scratch = [
        vmem((depth, 2 * width), bf16),
        vmem((width, depth), bf16),
        vmem((2, 2, NZ, 2, HALF, depth), bf16),
        vmem((2, NX, NY, HALF, 2 * width), bf16),
        vmem((2, NX, NY, HALF, width), bf16),
        vmem((2, NX, NY, HALF, 2 * width), f32),
        vmem((2, NX, NY, HALF, width), f32),
        vmem((2, 2, NX, HALF, 2 * width), bf16),
        vmem((2, 2, NX, HALF, width), bf16),
        vmem((2, NX, HALF, 2 * width), bf16),
        vmem((2, NX, HALF, width), bf16),
        vmem((2, NX, HALF, 2 * width), bf16),
        vmem((2, NX, HALF, width), bf16),
        vmem((2, NX - 1, HALF, 2 * width), bf16),
        vmem((2, NX - 1, HALF, width), bf16),
        vmem((2, HALF, 2 * width), f32),
        vmem((2, HALF, width), f32),
        vmem((2, HALF, 2 * width), f32),
        vmem((2, NX, NY, HALF, width), bf16),
        vmem((2, NX, NY, HALF, 2 * width), bf16),
        vmem((2, 2, NZ, 2, HALF, depth), f32),
        vmem((2, 2, NZ, HALF, depth), f32),
        vmem((2, 2, NZ, HALF, depth), bf16),
        vmem((2, 2, NZ, HALF, depth), bf16),
        vmem((2, 2, HALF, depth), f32),
        dma((7,)),
    ]
    scratch += [dma(shapes[kind]) for kind in KINDS for shapes in (DEPARTURES, ARRIVALS)]
    both_out = pl.pallas_call(
        functools.partial(kernel, split),
        name="swiglu_both_ways",
        out_shape=jax.ShapeDtypeStruct((2, 2, HALF, depth), bf16),
        in_specs=[pl.BlockSpec(memory_space=pl.ANY)] * 5,
        out_specs=pl.BlockSpec(memory_space=pltpu.VMEM),
        scratch_shapes=scratch,
        compiler_params=pltpu.CompilerParams(
            collective_id=0, has_side_effects=True, vmem_limit_bytes=60 << 20
        ),
    )(
        tokens.reshape(2, HALF, depth),
        cotangent.reshape(2, HALF, depth),
        gate_weight,
        up_weight,
        down_weight,
    )
    shape = jax.ShapeDtypeStruct((rows, depth), bf16)
    return pl.pallas_call(
        finish,
        name="finish",
        out_shape=(shape, shape),
        in_specs=[pl.BlockSpec(memory_space=pltpu.VMEM)],
        out_specs=(pl.BlockSpec(memory_space=pltpu.VMEM),) * 2,
    )(both_out.reshape(2, rows, depth))


def solution(mesh):
    placed = (P("col", "row"), P("col", "row"), P("row", "col"), P("row", "col"), P("col", "row"))
    return jax.shard_map(
        body,
        mesh=mesh,
        in_specs=placed,
        out_specs=(P("col", "row"), P("col", "row")),
        check_vma=False,
    )
```

```python
import functools

import jax
import jax.numpy as jnp
from jax import lax
from jax.experimental import pallas as pl
from jax.experimental.pallas import tpu as pltpu
from jax.sharding import PartitionSpec as P

MESH = pl.DeviceIdType.MESH
NX, NY, NZ = 4, 4, 8
NB = NX * NY
HALF = 16
TILE = 256
PARTS = 4
GROUPS = (
    ((0, 2, 0, 0), (2, 2, -1, 0), (4, 2, 1, 0), (6, 1, 2, 0), (7, 1, -2, 0)),
    ((0, 1, 2, 1), (1, 1, -2, 1), (2, 2, 3, 0), (4, 2, -3, 0), (6, 2, 4, 0)),
)
NEAR, FAR = 0, 1
OTHERS = (pl.ds(2, 6), pl.ds(0, 8))
ARRIVALS = {
    "seen": (2, 2),
    "share": (2, 2),
    "relay": (2, 2, PARTS),
    "rs1": (2, 2, PARTS),
    "rs2": (2, 2, PARTS),
    "ag1": (2, 2, PARTS),
    "ag1on": (2, 2, PARTS),
    "first": (2, 2, PARTS),
    "rest": (2, 2, PARTS),
    "pair": (2, 2, 2),
    "z": (2, 2, 2),
}
KINDS = tuple(ARRIVALS)
DEPARTURES = {kind: (2, 2) if kind in ("seen", "share", "z") else (2,) for kind in KINDS}
LAST = (0, 0)
STRIPS = ((2, 2), (2, 2))
SCHEDULE = (
    ("gs", 0, 0), ("gs", 1, 0), ("gs", 0, 1), ("gs", 1, 1), ("gw", 0, 0), ("b", 0, 0, 2),
    ("b", 0, 0, 1), ("b", 0, 0, 0), ("b", 0, 0, 3), ("b2", 0, 0, 2), ("b2", 0, 0, 0),
    ("b2", 0, 0, 1), ("gw", 1, 0), ("b2", 0, 0, 3), ("r", 0, 0, 2), ("b", 1, 0, 1),
    ("r", 0, 0, 1), ("r", 0, 0, 0), ("r", 0, 0, 3), ("b2", 1, 0, 1), ("b", 1, 0, 2),
    ("b", 1, 0, 0), ("b2", 1, 0, 0), ("b", 1, 0, 3), ("b2", 1, 0, 3), ("r", 1, 0, 1),
    ("s1", 0, 0, 2), ("gw", 0, 1), ("s1", 0, 0, 1), ("s1", 0, 0, 0), ("s1", 0, 0, 3),
    ("b", 0, 1, 1), ("b", 0, 1, 2), ("b", 0, 1, 3), ("b", 0, 1, 0), ("s1", 1, 0, 1),
    ("b2", 0, 1, 1), ("r", 1, 0, 0), ("b2", 0, 1, 0), ("b2", 0, 1, 2), ("r", 0, 1, 1),
    ("s2", 0, 0, 3), ("r", 0, 1, 2), ("r", 0, 1, 3), ("s2", 0, 0, 1), ("gw", 1, 1),
    ("b2", 0, 1, 3), ("r", 0, 1, 0), ("s2", 0, 0, 0), ("s2", 0, 0, 2), ("b", 1, 1, 1),
    ("b", 1, 1, 2), ("b", 1, 1, 3), ("b2", 1, 1, 3), ("s1", 0, 1, 1), ("s1", 0, 1, 2),
    ("b2", 1, 1, 2), ("b", 1, 1, 0), ("g0", 0, 0, 3), ("s1", 0, 1, 0), ("g0", 0, 0, 0),
    ("s1", 0, 1, 3), ("r", 1, 1, 1), ("r", 1, 1, 2), ("g0", 0, 0, 2), ("b2", 1, 1, 0),
    ("b2", 1, 1, 1), ("r", 1, 1, 3), ("s2", 0, 1, 1), ("g0", 0, 0, 1), ("s2", 0, 1, 2),
    ("r", 1, 0, 3), ("r", 1, 1, 0), ("g1", 0, 0, 0), ("g1", 0, 0, 3), ("s2", 0, 1, 0),
    ("s1", 1, 1, 2), ("g1", 0, 0, 2), ("s2", 0, 1, 3), ("s1", 1, 1, 1), ("s1", 1, 1, 3),
    ("g0", 0, 1, 2), ("b2", 1, 0, 2), ("s1", 1, 0, 0), ("s1", 1, 1, 0), ("g0", 0, 1, 1),
    ("g1", 0, 0, 1), ("r", 1, 0, 2), ("g0", 0, 1, 0), ("g2", 0, 0, 3), ("s2", 1, 1, 2),
    ("g2", 0, 0, 0), ("g0", 0, 1, 3), ("s2", 1, 1, 1), ("s2", 1, 1, 3), ("g1", 0, 1, 2),
    ("g2", 0, 0, 2), ("g1", 0, 1, 1), ("g2", 0, 0, 1), ("s2", 1, 1, 0), ("g1", 0, 1, 0),
    ("g0", 1, 1, 2), ("f", 0, 0, 1, 3), ("g1", 0, 1, 3), ("f", 0, 0, 1, 0), ("g0", 1, 1, 3),
    ("s1", 1, 0, 2), ("s2", 1, 0, 0), ("s1", 1, 0, 3), ("g2", 0, 1, 1), ("f", 0, 0, 0, 0),
    ("g0", 1, 1, 1), ("g2", 0, 1, 2), ("f", 0, 0, 0, 3), ("s2", 1, 0, 1), ("f", 0, 0, 1, 2),
    ("f", 0, 0, 0, 2), ("f", 0, 0, 0, 1), ("g0", 1, 1, 0), ("p", 0, 0, 0), ("f", 0, 0, 1, 1),
    ("g2", 0, 1, 0), ("p", 0, 0, 1), ("g1", 1, 1, 2), ("g2", 0, 1, 3), ("g1", 1, 1, 3),
    ("f", 0, 1, 1, 1), ("z", 0, 0, 0), ("s2", 1, 0, 2), ("s2", 1, 0, 3), ("z", 0, 0, 1),
    ("g1", 1, 1, 0), ("g1", 1, 1, 1), ("f", 0, 1, 1, 2), ("f", 0, 1, 1, 0), ("g0", 1, 0, 1),
    ("f", 0, 1, 1, 3), ("p", 0, 1, 1), ("g0", 1, 0, 0), ("g2", 1, 1, 3), ("f", 0, 1, 0, 3),
    ("f", 0, 1, 0, 0), ("f", 0, 1, 0, 1), ("z", 0, 1, 1), ("g2", 1, 1, 2), ("g0", 1, 0, 3),
    ("g0", 1, 0, 2), ("g2", 1, 1, 0), ("g2", 1, 1, 1), ("f", 0, 1, 0, 2), ("p", 0, 1, 0),
    ("g1", 1, 0, 0), ("g1", 1, 0, 1), ("z", 0, 1, 0), ("f", 1, 1, 1, 2), ("g1", 1, 0, 3),
    ("g1", 1, 0, 2), ("f", 1, 1, 1, 3), ("f", 1, 1, 0, 2), ("f", 1, 1, 1, 1),
    ("f", 1, 1, 1, 0), ("p", 1, 1, 1), ("g2", 1, 0, 1), ("g2", 1, 0, 0), ("z", 1, 1, 1),
    ("f", 1, 1, 0, 3), ("f", 1, 1, 0, 0), ("g2", 1, 0, 3), ("g2", 1, 0, 2), ("f", 1, 1, 0, 1),
    ("p", 1, 1, 0), ("f", 1, 0, 1, 1), ("f", 1, 0, 0, 1), ("z", 1, 1, 0), ("out", 0, 1, 1),
    ("f", 1, 0, 0, 0), ("out", 0, 1, 0), ("f", 1, 0, 1, 3), ("f", 1, 0, 0, 3),
    ("f", 1, 0, 0, 2), ("p", 1, 0, 0), ("f", 1, 0, 1, 2), ("out", 0, 0, 0), ("f", 1, 0, 1, 0),
    ("p", 1, 0, 1), ("z", 1, 0, 0), ("z", 1, 0, 1), ("out", 0, 0, 1), ("out", 1, 1, 1),
    ("out", 1, 1, 0), ("out", 1, 0, 0), ("out", 1, 0, 1),
)


def kernel(
    widths,
    tokens,
    cotangent,
    gate_weight,
    up_weight,
    down_weight,
    both_out,
    gu_w,
    down_w,
    seen,
    send1_p,
    send1_q,
    full_p,
    full_q,
    recv1_p,
    recv1_q,
    relay_p,
    relay_q,
    send2_p,
    send2_q,
    recv2_p,
    recv2_q,
    own2_p,
    own2_q,
    gate_up,
    hidden,
    grads,
    acc,
    pair,
    zsend,
    zrecv,
    result,
    load_sem,
    *sems,
):
    row, col = lax.axis_index("row"), lax.axis_index("col")
    x, y = row // NY, row % NY
    z, k = col // 2, col % 2

    def at(dx=0, dy=0, dz=0, dk=0):
        return (
            ((x + dx) % NX) * NY + (y + dy) % NY,
            ((z + dz) % NZ) * 2 + (k + dk) % 2,
        )

    def remote(src, dst, kind, index, device):
        send, recv = sems[2 * KINDS.index(kind)], sems[2 * KINDS.index(kind) + 1]
        return pltpu.make_async_remote_copy(
            src_ref=src,
            dst_ref=dst,
            send_sem=send.at[index[: len(DEPARTURES[kind])]],
            recv_sem=recv.at[index],
            device_id=device,
            device_id_type=MESH,
        )

    def arrive(like, kind, index):
        remote(like, like, kind, index, at(dk=1)).wait_recv()

    def depart(like, kind, index):
        index = (*index, 0, 0)[: len(ARRIVALS[kind])]
        remote(like, like, kind, index, at(dk=1)).wait_send()

    offset = tuple(sum(widths[:o]) for o in range(PARTS))
    span1 = tuple(pl.ds(offset[o], widths[o]) for o in range(PARTS))
    span2 = tuple(pl.ds(2 * offset[o], 2 * widths[o]) for o in range(PARTS))

    loads = [
        pltpu.make_async_copy(src, dst, load_sem.at[i])
        for i, (src, dst) in enumerate(
            [(tokens, seen.at[0, NEAR, pl.ds(0, 2), k]), (cotangent, seen.at[1, NEAR, pl.ds(0, 2), k])]
            + [
                (
                    src.at[:, span1[o]],
                    gu_w.at[:, pl.ds(2 * offset[o] + p * widths[o], widths[o])],
                )
                for o in range(PARTS)
                for p, src in enumerate((gate_weight, up_weight))
            ]
            + [(down_weight, down_w)]
        )
    ]

    barrier = pltpu.get_barrier_semaphore()
    friends = (
        [at(dx=d) for d in range(1, NX)]
        + [at(dy=d) for d in range(1, NY)]
        + [at(dz=d) for d in range(1, NZ)]
        + [at(dk=1)]
    )
    for friend in friends:
        pl.semaphore_signal(barrier, inc=1, device_id=friend, device_id_type=MESH)
    for load in loads:
        load.start()
    pl.semaphore_wait(barrier, len(friends))

    def go(copy):
        copy.start()

    def own_block(t, n, h):
        return (tokens, cotangent)[t].at[pl.ds(h, n)]

    def step_gs(t, g):
        for j, n, dz, h in GROUPS[g]:
            block = seen.at[t, g, pl.ds(j, n), k]
            if dz:
                go(remote(own_block(t, n, h), block, "seen", (t, g), at(dz=-dz)))
        if g == NEAR:
            own = seen.at[t, g, pl.ds(0, 2), k]
            go(remote(own_block(t, 2, 0), own, "share", (t, g), at(dk=1)))

    def step_gw(t, g):
        block = seen.at[t, g, OTHERS[g], k]
        arrive(block, "seen", (t, g))
        go(remote(block, block, "share", (t, g), at(dk=1)))

    def product(left, weight, turned, full, send, g, start, extent):
        def tile(first, size):
            cols = pl.ds(first, size)
            if turned:
                term = lax.dot_general(
                    left, weight[cols, :], (((1,), (1,)), ((), ())),
                    preferred_element_type=jnp.float32,
                )
            else:
                term = jnp.dot(left, weight[:, cols], preferred_element_type=jnp.float32)
            term = term.reshape(NX, NY, HALF, size)
            full[g, :, :, :, cols] = term
            send[g, :, :, :, cols] = term.astype(jnp.bfloat16)

        for first in range(start, start + extent, TILE):
            tile(first, min(TILE, start + extent - first))

    kinds = (
        (span2, full_p, send1_p, recv1_p, relay_p, send2_p, recv2_p, own2_p),
        (span1, full_q, send1_q, recv1_q, relay_q, send2_q, recv2_q, own2_q),
    )
    low, high, whole = pl.ds(0, NX // 2), pl.ds(NX // 2, NX // 2), pl.ds(0, NX)

    def along_x(g, o):
        return (g + o) % 2 == 0

    def line(g, o, step):
        if along_x(g, o):
            return at(dx=step), (x + step) % NX
        return at(dy=step), (y + step) % NY

    def cross(g, o, step):
        return line(g + 1, o, step)

    def part(buf, g, o, chunk, inner, cols):
        if along_x(g, o):
            return buf.at[g, chunk, inner, :, cols]
        return buf.at[g, inner, chunk, :, cols]

    def rs1_copies(q, g, o):
        span, _, send1, recv1, relay, _, _, _ = kinds[q]
        (right, after), (left, before) = line(g, o, 1), line(g, o, -1)
        _, opposite = line(g, o, 2)
        plan = [
            ("relay", right, opposite, low, relay.at[g, low, :, span[o]]),
            ("relay", left, opposite, high, relay.at[g, high, :, span[o]]),
            ("rs1", right, after, high, recv1.at[g, 0, high, :, span[o]]),
            ("rs1", left, before, low, recv1.at[g, 1, low, :, span[o]]),
            ("rs1", right, after, low, recv1.at[g, 0, low, :, span[o]]),
            ("rs1", left, before, high, recv1.at[g, 1, high, :, span[o]]),
        ]
        return [
            remote(part(send1, g, o, chunk, inner, span[o]), dst, kind, (q, g, o), device)
            for kind, device, chunk, inner, dst in plan
        ]

    arrived = set()

    def once(key, wait):
        if key not in arrived:
            arrived.add(key)
            wait()

    def tokens_there(q, g):
        arrive(seen.at[q, g, :, k], "share", (q, g))
        if g == NEAR:
            loads[q].wait()

    def step_b(q, g, o):
        once(("seen", q, g), lambda: tokens_there(q, g))
        for n in (2 + 2 * PARTS,) if q else (2 + 2 * o, 3 + 2 * o):
            once(("load", n), loads[n].wait)
        left = seen[q, g].reshape(NB * HALF, seen.shape[-1])
        if q == 0:
            product(left, gu_w, False, full_p, send1_p, g, 2 * offset[o], 2 * widths[o])
        else:
            product(left, down_w, True, full_q, send1_q, g, offset[o], widths[o])
        for copy in rs1_copies(q, g, o)[:2]:
            go(copy)

    def step_b2(q, g, o):
        for copy in rs1_copies(q, g, o)[2:4]:
            go(copy)

    def step_r(q, g, o):
        span, full, send1, _, relay, _, _, _ = kinds[q]
        copies = rs1_copies(q, g, o)
        arrive(relay.at[g, :, :, span[o]], "relay", (q, g, o))
        for side, blocks in enumerate((range(NX // 2), range(NX // 2, NX))):
            _, chunk = line(g, o, 1 - 2 * side)
            for i in blocks:
                total = part(full, g, o, chunk, i, span[o])[...]
                total += relay[g, i, :, span[o]].astype(jnp.float32)
                part(send1, g, o, chunk, i, span[o])[...] = total.astype(jnp.bfloat16)
            go(copies[side - 2])

    def rs2_copies(q, g, o):
        span, _, _, _, _, send2, recv2, _ = kinds[q]
        return [
            remote(
                send2.at[g, cross(g, o, d)[1], :, span[o]],
                recv2.at[g, d - 1, :, span[o]],
                "rs2",
                (q, g, o),
                cross(g, o, d)[0],
            )
            for d in range(1, NX)
        ]

    def step_s1(q, g, o):
        span, full, _, recv1, _, send2, _, own2 = kinds[q]
        arrive(recv1.at[g, :, :, :, span[o]], "rs1", (q, g, o))

        def total(i):
            mine = part(full, g, o, line(g, o, 0)[1], i, span[o])[...]
            for d in range(2):
                mine += recv1[g, d, i, :, span[o]].astype(jnp.float32)
            return mine

        for i in range(NX):
            send2[g, i, :, span[o]] = total(i).astype(jnp.bfloat16)
        own2[g, :, span[o]] = total(cross(g, o, 0)[1])
        for copy in rs2_copies(q, g, o):
            go(copy)

    def ag_bufs(q):
        return (hidden, span1) if q == 0 else (grads, span2)

    def spot(g, o, step):
        device, place = cross(g, o, step)
        return device, (x, place) if along_x(g, o) else (place, y)

    def ag1_start(q, g, o):
        buf, span = ag_bufs(q)
        mine = buf.at[g, x, y, :, span[o]]
        for step in (1, -1):
            go(remote(mine, mine, "ag1", (q, g, o), spot(g, o, step)[0]))

    def step_g0(q, g, o):
        buf, span = ag_bufs(q)
        arrive(buf.at[g, 0, pl.ds(0, 2), :, span[o]], "ag1", (q, g, o))
        head = (span[o].size // 128 + 1) // 2 * 128
        for step, start, size in ((1, 0, head), (-1, head, span[o].size - head)):
            block = buf.at[(g, *spot(g, o, -step)[1], slice(None), pl.ds(span[o].start + start, size))]
            go(remote(block, block, "ag1on", (q, g, o), spot(g, o, step)[0]))

    def ag2_copies(q, g, o):
        buf, span = ag_bufs(q)
        (right, after), (left, before) = line(g, o, 1), line(g, o, -1)
        _, mine = line(g, o, 0)
        plan = [
            ("first", right, mine, low),
            ("first", left, mine, high),
            ("rest", right, mine, high),
            ("rest", left, mine, low),
            ("rest", right, before, low),
            ("rest", left, after, high),
        ]
        return [
            remote(
                part(buf, g, o, chunk, inner, span[o]),
                part(buf, g, o, chunk, inner, span[o]),
                kind,
                (q, g, o),
                device,
            )
            for kind, device, chunk, inner in plan
        ]

    def step_s2(q, g, o):
        span, _, _, _, _, _, recv2, own2 = kinds[q]
        arrive(recv2.at[g, :, :, span[o]], "rs2", (q, g, o))
        total = own2[g, :, span[o]]
        for d in range(NX - 1):
            total += recv2[g, d, :, span[o]].astype(jnp.float32)
        first, second = (
            pl.ds(2 * offset[o], widths[o]),
            pl.ds(2 * offset[o] + widths[o], widths[o]),
        )
        if q == 0:
            gate_up[g, :, span[o]] = total
            gate, up = total[:, : widths[o]], total[:, widths[o] :]
            hidden[g, x, y, :, span1[o]] = (gate * jax.nn.sigmoid(gate) * up).astype(
                jnp.bfloat16
            )
        else:
            gate, up = gate_up[g, :, first], gate_up[g, :, second]
            sigmoid = jax.nn.sigmoid(gate)
            grads[g, x, y, :, first] = (
                total * up * sigmoid * (1.0 + gate * (1.0 - sigmoid))
            ).astype(jnp.bfloat16)
            grads[g, x, y, :, second] = (total * gate * sigmoid).astype(jnp.bfloat16)
        ag1_start(q, g, o)

    def step_g1(q, g, o):
        buf, span = ag_bufs(q)
        arrive(buf.at[g, 0, 0, :, span[o]], "ag1on", (q, g, o))
        for copy in ag2_copies(q, g, o)[:4]:
            go(copy)

    def step_g2(q, g, o):
        buf, span = ag_bufs(q)
        arrive(buf.at[g, 0, :, :, span[o]], "first", (q, g, o))
        for copy in ag2_copies(q, g, o)[4:]:
            go(copy)

    depth = down_w.shape[1]

    def strip_of(q, g, c):
        size = depth // STRIPS[q][g]
        return pl.ds(c * size, size)

    def pair_copy(t, g, c):
        return remote(
            acc.at[t, g, :, 1 - k, :, strip_of(t, g, c)],
            pair.at[t, g, :, :, strip_of(t, g, c)],
            "pair",
            (t, g, c),
            at(dk=1),
        )

    def step_f(q, g, c, o):
        buf, span = ag_bufs(q)
        once(
            ("rows", q, g, o),
            lambda: arrive(buf.at[g, pl.ds(0, 2), :, :, span[o]], "rest", (q, g, o)),
        )
        left = buf[g, :, :, :, span[o]].reshape(NB * HALF, span[o].size)
        strip = strip_of(q, g, c)
        more = ("part", q, g, c) in arrived
        arrived.add(("part", q, g, c))
        for n in range(strip.size // TILE):
            cols = pl.ds(strip.start + n * TILE, TILE)
            if q == 0:
                term = jnp.dot(left, down_w[span[o], cols], preferred_element_type=jnp.float32)
            else:
                term = lax.dot_general(
                    left, gu_w[cols, span[o]], (((1,), (1,)), ((), ())),
                    preferred_element_type=jnp.float32,
                )
            term = term.reshape(NZ, 2, HALF, TILE)
            acc[q, g, :, :, :, cols] = acc[q, g, :, :, :, cols] + term if more else term

    def step_p(q, g, c):
        go(pair_copy(q, g, c))

    def z_copy(t, g, c, e):
        j, n, dz, _ = GROUPS[g][e]
        runs = pl.ds(j, n)
        return remote(
            zsend.at[t, g, runs, :, strip_of(t, g, c)],
            zrecv.at[t, g, runs, :, strip_of(t, g, c)],
            "z",
            (t, g, c),
            at(dz=dz),
        )

    def step_z(t, g, c):
        pair_copy(t, g, c).wait_recv()

        @pl.loop(0, NZ)
        def _(i):
            zsend[t, g, i, :, strip_of(t, g, c)] = (
                acc[t, g, i, k, :, strip_of(t, g, c)] + pair[t, g, i, :, strip_of(t, g, c)]
            ).astype(jnp.bfloat16)

        for e, (_, _, dz, _) in sorted(enumerate(GROUPS[g]), key=lambda run: -abs(run[1][2])):
            if dz:
                go(z_copy(t, g, c, e))

    def step_out(t, g, c):
        cols = strip_of(t, g, c)
        last = g == LAST[t]
        total = [result[t, h, :, cols] if last else None for h in range(2)]
        if g == NEAR:
            for h in range(2):
                own = acc[t, g, h, k, :, cols] + pair[t, g, h, :, cols]
                total[h] = own if total[h] is None else total[h] + own
        arrive(zrecv.at[t, g, OTHERS[g], :, cols], "z", (t, g, c))
        for j, n, dz, first in GROUPS[g]:
            if dz:
                for i in range(n):
                    h = first + i
                    term = zrecv[t, g, j + i, :, cols].astype(jnp.float32)
                    total[h] = term if total[h] is None else total[h] + term
        for h in range(2):
            if last:
                both_out[t, h, :, cols] = total[h].astype(jnp.bfloat16)
            else:
                result[t, h, :, cols] = total[h]

    steps = {
        "gs": step_gs,
        "gw": step_gw,
        "b": step_b,
        "b2": step_b2,
        "r": step_r,
        "s1": step_s1,
        "s2": step_s2,
        "g0": step_g0,
        "g1": step_g1,
        "p": step_p,
        "g2": step_g2,
        "f": step_f,
        "z": step_z,
        "out": step_out,
    }
    for step, *where in SCHEDULE:
        steps[step](*where)

    for q in range(2):
        _, _, _, recv1, relay, _, recv2, _ = kinds[q]
        buf, _ = ag_bufs(q)
        for g in range(2):
            depart(seen.at[q, g, OTHERS[g], k], "seen", (q, g))
            depart(seen.at[q, g, :, k], "share", (q, g))
            depart(zrecv.at[q, g, OTHERS[g]], "z", (q, g))
        depart(relay, "relay", (q,))
        depart(recv1, "rs1", (q,))
        depart(recv2, "rs2", (q,))
        depart(buf.at[:, 0, pl.ds(0, 2)], "ag1", (q,))
        depart(buf.at[:, 0, 0], "ag1on", (q,))
        depart(buf.at[:, 0], "first", (q,))
        depart(buf.at[:, pl.ds(0, 2)], "rest", (q,))
        depart(pair.at[q], "pair", (q,))


def finish(both_out, output, input_grad):
    output[...] = both_out[0]
    input_grad[...] = both_out[1]


def body(tokens, cotangent, gate_weight, up_weight, down_weight):
    rows, depth = tokens.shape
    width = gate_weight.shape[1]
    lanes, more = divmod(width // 128, PARTS)
    widths = tuple(128 * (lanes + (o < more)) for o in range(PARTS))
    bf16, f32, dma = jnp.bfloat16, jnp.float32, pltpu.SemaphoreType.DMA
    vmem = pltpu.VMEM
    assert rows == 2 * HALF
    scratch = [
        vmem((depth, 2 * width), bf16),
        vmem((width, depth), bf16),
        vmem((2, 2, NZ, 2, HALF, depth), bf16),
        vmem((2, NX, NY, HALF, 2 * width), bf16),
        vmem((2, NX, NY, HALF, width), bf16),
        vmem((2, NX, NY, HALF, 2 * width), f32),
        vmem((2, NX, NY, HALF, width), f32),
        vmem((2, 2, NX, HALF, 2 * width), bf16),
        vmem((2, 2, NX, HALF, width), bf16),
        vmem((2, NX, HALF, 2 * width), bf16),
        vmem((2, NX, HALF, width), bf16),
        vmem((2, NX, HALF, 2 * width), bf16),
        vmem((2, NX, HALF, width), bf16),
        vmem((2, NX - 1, HALF, 2 * width), bf16),
        vmem((2, NX - 1, HALF, width), bf16),
        vmem((2, HALF, 2 * width), f32),
        vmem((2, HALF, width), f32),
        vmem((2, HALF, 2 * width), f32),
        vmem((2, NX, NY, HALF, width), bf16),
        vmem((2, NX, NY, HALF, 2 * width), bf16),
        vmem((2, 2, NZ, 2, HALF, depth), f32),
        vmem((2, 2, NZ, HALF, depth), f32),
        vmem((2, 2, NZ, HALF, depth), bf16),
        vmem((2, 2, NZ, HALF, depth), bf16),
        vmem((2, 2, HALF, depth), f32),
        dma((3 + 2 * PARTS,)),
    ]
    scratch += [dma(shapes[kind]) for kind in KINDS for shapes in (DEPARTURES, ARRIVALS)]
    both_out = pl.pallas_call(
        functools.partial(kernel, widths),
        name="swiglu_both_ways",
        out_shape=jax.ShapeDtypeStruct((2, 2, HALF, depth), bf16),
        in_specs=[pl.BlockSpec(memory_space=pl.ANY)] * 5,
        out_specs=pl.BlockSpec(memory_space=pltpu.VMEM),
        scratch_shapes=scratch,
        compiler_params=pltpu.CompilerParams(
            collective_id=0, has_side_effects=True, vmem_limit_bytes=60 << 20
        ),
    )(
        tokens.reshape(2, HALF, depth),
        cotangent.reshape(2, HALF, depth),
        gate_weight,
        up_weight,
        down_weight,
    )
    shape = jax.ShapeDtypeStruct((rows, depth), bf16)
    return pl.pallas_call(
        finish,
        name="finish",
        out_shape=(shape, shape),
        in_specs=[pl.BlockSpec(memory_space=pltpu.VMEM)],
        out_specs=(pl.BlockSpec(memory_space=pltpu.VMEM),) * 2,
    )(both_out.reshape(2, rows, depth))


def solution(mesh):
    placed = (P("col", "row"), P("col", "row"), P("row", "col"), P("row", "col"), P("col", "row"))
    return jax.shard_map(
        body,
        mesh=mesh,
        in_specs=placed,
        out_specs=(P("col", "row"), P("col", "row")),
        check_vma=False,
    )
```
